512 devices in a mesh: seq: 128 (over z, x, y_hi, core), grp: 4 (over y_lo).
Axes of the slice: x: 4, y: 8 (y_hi: 2, y_lo: 4; y = y_hi * 4 + y_lo), z: 8, core: 2. Of those that a mesh axis runs over, the one named last changes fastest.
Arguments:
- signal: bfloat16 [4, 131072, 384], P('grp', 'seq'), may hold values from -6 to 6
- tap_weights: bfloat16 [3, 384, 384], replicated, may hold values from -0.1875 to 0.1875
- bias_inner: float32 [384], replicated, may hold values from -3 to 3
- w_out: bfloat16 [384, 384], replicated, may hold values from -0.3125 to 0.3125
- cotangent: bfloat16 [4, 131072, 384], P('grp', 'seq'), may hold values from -6 to 6
Outputs:
- output: bfloat16 [4, 131072, 384], P('grp', 'seq')
- grad_signal: bfloat16 [4, 131072, 384], P('grp', 'seq')
- grad_taps: bfloat16 [3, 384, 384], replicated
- grad_bias: float32 [384], replicated
- grad_out: bfloat16 [384, 384], replicated
The draws below stay inside these ranges and needn't reach their ends.
All inputs are finite; a program needn't handle non-finite values.
Results may differ from the reference program's by a relative error of at most 0.0075.
Values may be sent and summed in bfloat16 or wider, within the bound.
A program may use at most 64 MiB of HBM per device.

```python
import math
import jax
import jax.numpy as jnp
from jax import lax

C = 384
H = 384
TAPS = 3
DILATION_BINS = 4096
LEN = 131072
GROUPS = 4


def steps_of(own_key, shape, split, least, top_value):
    factor_of = 1.0
    for position, parts in split:
        draws = jax.random.uniform(jax.random.fold_in(jax.random.fold_in(own_key, 6), position), (parts,), jnp.float32, least / len(split), top_value / len(split))
        factor_of = factor_of * jnp.repeat(jnp.exp(draws), shape[position] // parts).reshape((-1,) + (1,) * (len(shape) - 1 - position))
    return factor_of


def bell_draw(own_key, shape, deviation, limit, pieces=(), held_as=jnp.bfloat16):
    entries = jax.random.normal(own_key, shape, jnp.float32) * deviation
    if len(pieces) > 0:
        entries = steps_of(own_key, shape, pieces, -0.22, 0.18) * entries
    return jnp.clip(entries, min=-limit, max=limit).astype(held_as)


def setup_inputs(seed: int = 0) -> dict:
    splits = jax.random.split(jax.random.key(seed), 6)
    signal = bell_draw(splits[0], (GROUPS, LEN, C), 1.0, 6.0, ((0, 4), (1, 128)))
    tap_weights = bell_draw(splits[1], (TAPS, C, H), (3 * C) ** -0.5, 0.1875)
    bias_inner = bell_draw(splits[2], (H,), 0.7, 3.0, (), jnp.float32)
    w_out = bell_draw(splits[3], (H, C), H ** -0.5, 0.3125)
    cotangent = bell_draw(splits[4], (GROUPS, LEN, C), 1.0, 6.0, ((0, 4), (1, 128)))
    return {"signal": signal, "tap_weights": tap_weights, "bias_inner": bias_inner, "w_out": w_out, "cotangent": cotangent}


def gelu_exact(value):
    return value * 0.5 * (1.0 + jax.scipy.special.erf(value / math.sqrt(2.0)))

def gelu_slope(value):
    normal_cdf = 0.5 * (1.0 + jax.scipy.special.erf(value / math.sqrt(2.0)))
    return normal_cdf + value * jnp.exp(-0.5 * value * value) / math.sqrt(2.0 * math.pi)

def displaced_signal(rows, offset):
    zeros = jnp.zeros((abs(offset), rows.shape[1]), rows.dtype)
    if offset > 0:
        return jnp.concatenate([rows[offset:], zeros], 0)
    return jnp.concatenate([zeros, rows[:offset]], 0)

def reference(signal, tap_weights, bias_inner, w_out, cotangent):
    outputs = []
    grads = []
    tap_sums = [jnp.zeros((C, H), jnp.float32) for tap in range(3)]
    out_sum = jnp.zeros((H, C), jnp.float32)
    bias_sum = jnp.zeros((H,), jnp.float32)
    for member in range(signal.shape[0]):
        wide_sig = signal[member].astype(jnp.float32)
        cot_rows = cotangent[member]
        gelu_output = gelu_exact(wide_sig).astype(jnp.bfloat16)
        leading_rows = displaced_signal(gelu_output, -DILATION_BINS)
        trailing_rows = displaced_signal(gelu_output, DILATION_BINS)
        pre_gate = bias_inner + jnp.dot(leading_rows, tap_weights[0], preferred_element_type=jnp.float32)
        pre_gate = pre_gate + jnp.dot(gelu_output, tap_weights[1], preferred_element_type=jnp.float32)
        pre_gate = pre_gate + jnp.dot(trailing_rows, tap_weights[2], preferred_element_type=jnp.float32)
        hidden = gelu_exact(pre_gate).astype(jnp.bfloat16)
        outputs.append((wide_sig + jnp.dot(hidden, w_out, preferred_element_type=jnp.float32)).astype(jnp.bfloat16))
        grad_hidden = jnp.dot(cot_rows, w_out.T, preferred_element_type=jnp.float32)
        preactivation_gradient = (grad_hidden * gelu_slope(pre_gate)).astype(jnp.bfloat16)
        activation_gradient = jnp.dot(displaced_signal(preactivation_gradient, DILATION_BINS), tap_weights[0].T, preferred_element_type=jnp.float32)
        activation_gradient = activation_gradient + jnp.dot(preactivation_gradient, tap_weights[1].T, preferred_element_type=jnp.float32)
        activation_gradient = activation_gradient + jnp.dot(displaced_signal(preactivation_gradient, -DILATION_BINS), tap_weights[2].T, preferred_element_type=jnp.float32)
        grads.append((cot_rows.astype(jnp.float32) + activation_gradient * gelu_slope(wide_sig)).astype(jnp.bfloat16))
        tap_sums[0] = tap_sums[0] + jnp.dot(leading_rows.T, preactivation_gradient, preferred_element_type=jnp.float32)
        tap_sums[1] = tap_sums[1] + jnp.dot(gelu_output.T, preactivation_gradient, preferred_element_type=jnp.float32)
        tap_sums[2] = tap_sums[2] + jnp.dot(trailing_rows.T, preactivation_gradient, preferred_element_type=jnp.float32)
        out_sum = out_sum + jnp.dot(hidden.T, cot_rows, preferred_element_type=jnp.float32)
        bias_sum = bias_sum + lax.optimization_barrier(jnp.sum(preactivation_gradient.astype(jnp.float32), 0))
    grad_taps = jnp.stack(tap_sums, 0).astype(jnp.bfloat16)
    return (jnp.stack(outputs, 0), jnp.stack(grads, 0), grad_taps, bias_sum, out_sum.astype(jnp.bfloat16))
```

```python
import functools
import math

import jax
import jax.numpy as jnp
from jax import lax
from jax.experimental import pallas as pl
from jax.experimental.pallas import tpu as pltpu
from jax.sharding import PartitionSpec as P

F32 = jnp.float32
BF16 = jnp.bfloat16
MESH = pl.DeviceIdType.MESH

NX = 4
NYH = 2
CHUNK = 128
SHARE = 48


def rows_dot(a, b):
    return lax.dot_general(a, b, (((1,), (0,)), ((), ())), preferred_element_type=F32)


def rows_dot_t(a, b):
    return lax.dot_general(a, b, (((1,), (1,)), ((), ())), preferred_element_type=F32)


def sum_rows_dot(a, b):
    return lax.dot_general(a, b, (((0,), (0,)), ((), ())), preferred_element_type=F32)


def cdf_of(v):
    return 0.5 * (1.0 + lax.erf(v * (1.0 / math.sqrt(2.0))))


def slope_of(v, cdf):
    return cdf + v * jnp.exp(-0.5 * v * v) * (1.0 / math.sqrt(2.0 * math.pi))


class Half:
    def __init__(self, start, piece, n_first, n_second, extra):
        self.start, self.piece = start, piece
        self.n_first, self.n_second = n_first, n_second
        pieces = piece // 8
        owners = max(n for n in range(1, n_second + 1 - extra) if pieces % n == 0)
        self.owned = piece // owners
        self.weight_owners = owners
        self.owners = owners + extra


def kernel(cfg, *refs):
    nz, ny, nyl, nc, ch, halves = cfg
    (sig_h, taps_h, bias_r, wout_h, cot_h, out_h, gsig_h, gtaps_h, gbias_r, gout_h,
     sig, cot, taps, wout, act, lead, trail, gp, gpl, gpr, outb, gsb, pre, gh, slope,
     acc, bacc, cs, cr, bcr, s1s_a, s1s_b, s1r_a, s1r_b, b1r, p_a, p_b, s2r_a, s2r_b, xs_a, xs_b, pf_a, pf_b, bfin, gall,
     in_sem, w_sem, out_sem, act_s, act_r, gp_s, gp_r, c_s, c_r, s1_s, s1_r, b1_s, b1_r, s2_s, s2_r,
     x_s, x_r, ag2_s, ag2_r, ag1_s, ag1_r, bag_s, bag_r, cag_s, cag_r) = refs
    s1s, s1r, pp, s2r, xs, pf = (s1s_a, s1s_b), (s1r_a, s1r_b), (p_a, p_b), (s2r_a, s2r_b), (xs_a, xs_b), (pf_a, pf_b)
    seq, grp = lax.axis_index("seq"), lax.axis_index("grp")
    hop = 2 * NYH
    core = seq % 2
    y = ((seq // 2) % NYH) * nyl + grp
    x = (seq // hop) % NX
    z = seq // (hop * NX)
    n_seq = nz * NX * hop
    has_right = seq + hop < n_seq
    has_left = seq >= hop
    right, left = (seq + hop, grp), (seq - hop, grp)
    other = (seq + 1 - 2 * core, grp)

    def y_peer(p):
        return (seq + (p // nyl - (seq // 2) % NYH) * 2, p % nyl)

    def z_peer(p):
        return (seq + (p - z) * (hop * NX), grp)

    def x_peer(p):
        return (seq + (p - x) * hop, grp)

    first, second = (y_peer, z_peer), (z_peer, y_peer)
    me_first, me_second = (y, z), (z, y)

    def remote(src, dst, send_sem, recv_sem, to):
        return pltpu.make_async_remote_copy(src_ref=src, dst_ref=dst, send_sem=send_sem, recv_sem=recv_sem,
                                            device_id=to, device_id_type=MESH)

    def ring(n, me, body):
        def step(k, carry):
            body(lax.rem(me + k, n))
            return carry
        lax.fori_loop(1, n, step, 0)

    def chunks(first_c, last_c, body):
        def step(c, carry):
            body(c)
            return carry
        lax.fori_loop(first_c, last_c, step, 0)

    def sig_copy(c):
        return pltpu.make_async_copy(sig_h.at[0, pl.ds(pl.multiple_of(c * ch, ch), ch)], sig.at[c], in_sem.at[c])

    def cot_copy(c):
        return pltpu.make_async_copy(cot_h.at[0, pl.ds(pl.multiple_of(c * ch, ch), ch)], cot.at[c], in_sem.at[nc + c])

    taps_copy = pltpu.make_async_copy(taps_h, taps, w_sem.at[0])
    wout_copy = pltpu.make_async_copy(wout_h, wout, w_sem.at[1])
    chunks(0, nc, lambda c: sig_copy(c).start())
    taps_copy.start()
    wout_copy.start()
    chunks(0, nc, lambda c: cot_copy(c).start())

    barrier = pltpu.get_barrier_semaphore()

    def greet(to):
        pl.semaphore_signal(barrier, inc=1, device_id=to, device_id_type=MESH)

    cross_right = jnp.logical_and(x == NX - 1, has_right)
    cross_left = jnp.logical_and(x == 0, has_left)
    ring(NX, x, lambda p: greet(x_peer(p)))
    pl.when(cross_right)(lambda: greet(right))
    pl.when(cross_left)(lambda: greet(left))
    greet(other)
    ring(ny, y, lambda p: greet(y_peer(p)))
    ring(nz, z, lambda p: greet(z_peer(p)))
    greeted = 1 + (NX - 1) + (ny - 1) + (nz - 1)

    def activate(c):
        sig_copy(c).wait()
        v = sig[c].astype(F32)
        act[c] = (v * cdf_of(v)).astype(BF16)

    def act_right(c):
        return remote(act.at[c], lead.at[c], act_s.at[c], act_r.at[c], right)

    def act_left(c):
        return remote(act.at[c], trail.at[c], act_s.at[nc + c], act_r.at[nc + c], left)

    def act_send(c):
        pl.when(has_right)(lambda: act_right(c).start())
        pl.when(has_left)(lambda: act_left(c).start())

    def gp_right(c):
        return remote(gp.at[c], gpl.at[c], gp_s.at[c], gp_r.at[c], right)

    def gp_left(c):
        return remote(gp.at[c], gpr.at[c], gp_s.at[nc + c], gp_r.at[nc + c], left)

    def gp_send(c):
        pl.when(has_right)(lambda: gp_right(c).start())
        pl.when(has_left)(lambda: gp_left(c).start())

    activate(0)
    pl.semaphore_wait(barrier, greeted + jnp.where(cross_right, 1, 0) + jnp.where(cross_left, 1, 0))
    act_send(0)

    def activate_send(c):
        activate(c)
        act_send(c)

    chunks(1, nc, activate_send)

    @pl.when(jnp.logical_not(has_left))
    def _():
        lead[...] = jnp.zeros_like(lead)
        gpl[...] = jnp.zeros_like(gpl)

    @pl.when(jnp.logical_not(has_right))
    def _():
        trail[...] = jnp.zeros_like(trail)
        gpr[...] = jnp.zeros_like(gpr)

    acc[...] = jnp.zeros_like(acc)
    bacc[...] = jnp.zeros_like(bacc)
    bias = bias_r[...].reshape(1, -1)
    taps_copy.wait()
    wout_copy.wait()

    def prepare(c):
        cot_copy(c).wait()
        pre[c] = bias + rows_dot(act[c], taps[1])
        gh[c] = rows_dot_t(cot[c], wout[...])
        v = sig[c].astype(F32)
        slope[c] = slope_of(v, cdf_of(v))

    chunks(0, nc, prepare)

    def act_wait(c):
        pl.when(has_left)(lambda: act_right(c).wait_recv())
        pl.when(has_right)(lambda: act_left(c).wait_recv())

    def out_copy(c):
        return pltpu.make_async_copy(outb.at[c], out_h.at[0, pl.ds(pl.multiple_of(c * ch, ch), ch)], out_sem.at[c])

    def gsig_copy(c):
        return pltpu.make_async_copy(gsb.at[c], gsig_h.at[0, pl.ds(pl.multiple_of(c * ch, ch), ch)], out_sem.at[nc + c])

    n_in = taps.shape[1]

    def add_rows(k, value):
        acc[k // 2, pl.ds((k % 2) * n_in, n_in)] += value

    def work(c):
        lead_c, trail_c, act_c, cot_c = lead[c], trail[c], act[c], cot[c]
        v = pre[c] + rows_dot(lead_c, taps[0]) + rows_dot(trail_c, taps[2])
        cdf = cdf_of(v)
        hidden = (v * cdf).astype(BF16)
        grad = (gh[c] * slope_of(v, cdf)).astype(BF16)
        gp[c] = grad
        outb[c] = (sig[c].astype(F32) + rows_dot(hidden, wout[...])).astype(BF16)
        out_copy(c).start()
        add_rows(0, sum_rows_dot(lead_c, grad))
        add_rows(1, sum_rows_dot(act_c, grad))
        add_rows(2, sum_rows_dot(trail_c, grad))
        add_rows(3, sum_rows_dot(hidden, cot_c))
        wide = grad.astype(F32)
        bacc[...] += jnp.sum(wide.reshape(ch // 8, 8, wide.shape[-1]), 0)

    def wait_work(c):
        act_wait(c)
        work(c)

    chunks(0, nc - 1, wait_work)
    act_wait(nc - 1)
    chunks(0, nc - 1, gp_send)
    work(nc - 1)
    gp_send(nc - 1)

    def core_copy(h):
        rows = pl.ds(halves[h].start, halves[h].piece * halves[h].n_first)
        return remote(cs.at[rows], cr.at[rows], c_s.at[h], c_r.at[h], other)

    bias_core = remote(bacc, bcr, c_s.at[2], c_r.at[2], other)
    for h in range(2):
        rows = pl.ds(halves[h].start, halves[h].piece * halves[h].n_first)
        cs[rows] = acc[1 - core, rows].astype(BF16)
        core_copy(h).start()
    bias_core.start()

    zb = nz - 1

    def s1_copy(h, p, sender):
        return remote(s1s[h].at[p], s1r[h].at[sender], s1_s.at[h, p], s1_r.at[h, sender], first[h](p))

    def b1_copy(sender):
        return remote(bfin.at[0], b1r.at[sender], b1_s, b1_r.at[sender], z_peer(zb))

    for h in range(2):
        core_copy(h).wait_recv()
        hf = halves[h]

        def add_piece(p, h=h, hf=hf):
            rows = pl.ds(pl.multiple_of(hf.start + p * hf.piece, 16), hf.piece)
            total = acc[core, rows] + cr[rows].astype(F32)
            acc[core, rows] = total
            s1s[h][p] = total.astype(BF16)

        def add_send(p, h=h):
            add_piece(p)
            s1_copy(h, p, me_first[h]).start()

        ring(hf.n_first, me_first[h], add_send)
        add_piece(me_first[h])
    bias_core.wait_recv()
    bfin[0] = bacc[...] + bcr[...]
    pl.when(z != zb)(lambda: b1_copy(z).start())

    def adjoint(c):
        pl.when(has_left)(lambda: gp_right(c).wait_recv())
        pl.when(has_right)(lambda: gp_left(c).wait_recv())
        grad = rows_dot_t(gp[c], taps[1]) + rows_dot_t(gpr[c], taps[0]) + rows_dot_t(gpl[c], taps[2])
        gsb[c] = (cot[c].astype(F32) + grad * slope[c]).astype(BF16)
        gsig_copy(c).start()

    chunks(0, 3, adjoint)

    def s2_copy(h, q, sender):
        n = halves[h].owned
        return remote(pp[h].at[pl.ds(pl.multiple_of(q * n, 8), n)], s2r[h].at[sender], s2_s.at[h, q], s2_r.at[h, sender], second[h](q))

    for h in range(2):
        hf = halves[h]
        rows = pl.ds(pl.multiple_of(hf.start + me_first[h] * hf.piece, 16), hf.piece)
        pp[h][pl.ds(0, hf.piece)] = acc[core, rows]

        def take(p, h=h, hf=hf):
            s1_copy(h, me_first[h], p).wait_recv()
            pp[h][pl.ds(0, hf.piece)] += s1r[h][p].astype(F32)

        ring(hf.n_first, me_first[h], take)
        if hf.owners > hf.weight_owners:
            spare = pl.ds(hf.piece, hf.owned)
            pp[h][spare] = jnp.zeros((hf.owned, acc.shape[-1]), F32)

            @pl.when(z == zb)
            def _(h=h, hf=hf):
                head = pl.ds(hf.piece, 8)
                pp[h][head] = bfin[0]

                def take_bias(p):
                    b1_copy(p).wait_recv()
                    pp[h][head] += b1r[p]

                ring(nz, z, take_bias)

        def scatter(q, h=h, hf=hf):
            pl.when(q < hf.owners)(lambda: s2_copy(h, q, me_second[h]).start())

        ring(hf.n_second, me_second[h], scatter)

    def x_copy(h, p, sender):
        return remote(xs[h].at[sender], xs[h].at[sender], x_s.at[h, p], x_r.at[h, sender], x_peer(p))

    for h in range(2):
        hf = halves[h]

        @pl.when(me_second[h] < hf.owners)
        def _(h=h, hf=hf):
            rows = pl.ds(pl.multiple_of(me_second[h] * hf.owned, 8), hf.owned)
            xs[h][x] = pp[h][rows]

            def take(p):
                s2_copy(h, me_second[h], p).wait_recv()
                xs[h][x] += s2r[h][p]

            ring(hf.n_second, me_second[h], take)
            ring(NX, x, lambda p: x_copy(h, p, x).start())

    def ag2_copy(h, p, sender):
        n = halves[h].owned
        rows = pl.ds(pl.multiple_of(sender * n, 8), n)
        return remote(pf[h].at[rows], pf[h].at[rows], ag2_s.at[h, p], ag2_r.at[h, sender], second[h](p))

    for h in range(2):
        hf = halves[h]

        @pl.when(me_second[h] < hf.owners)
        def _(h=h, hf=hf):
            ring(NX, x, lambda p: x_copy(h, x, p).wait_recv())
            total = xs[h][0]
            for p in range(1, NX):
                total = total + xs[h][p]
            pf[h][pl.ds(pl.multiple_of(me_second[h] * hf.owned, 8), hf.owned)] = total
            ring(hf.n_second, me_second[h], lambda p: ag2_copy(h, p, me_second[h]).start())

    def piece_of(h, p):
        return pl.ds(pl.multiple_of(halves[h].start + p * halves[h].piece, 16), halves[h].piece)

    def ag1_copy(h, p, sender):
        ref = gall.at[core, piece_of(h, sender)]
        return remote(ref, ref, ag1_s.at[h, p], ag1_r.at[h, sender], first[h](p))

    def cag_copy(h, p, side):
        ref = gall.at[side, piece_of(h, p)]
        return remote(ref, ref, cag_s.at[h, p], cag_r.at[h, p], other)

    def bag_copy(p):
        return remote(bfin.at[1], bfin.at[1], bag_s.at[p], bag_r, z_peer(p))

    for h in range(2):
        hf = halves[h]

        def take(q, h=h, hf=hf):
            pl.when(q < hf.owners)(lambda: ag2_copy(h, me_second[h], q).wait_recv())

        ring(hf.n_second, me_second[h], take)
        gall[core, piece_of(h, me_first[h])] = pf[h][pl.ds(0, hf.piece)].astype(BF16)
        ring(hf.n_first, me_first[h], lambda p, h=h: ag1_copy(h, p, me_first[h]).start())
        cag_copy(h, me_first[h], core).start()
        if hf.owners > hf.weight_owners:

            @pl.when(z == zb)
            def _(h=h, hf=hf):
                bfin[1] = pf[h][pl.ds(hf.piece, 8)]
                ring(nz, z, lambda p: bag_copy(p).start())

    chunks(3, nc, adjoint)

    for h in range(2):
        hf = halves[h]

        def pass_on(p, h=h):
            ag1_copy(h, me_first[h], p).wait_recv()
            cag_copy(h, p, core).start()

        ring(hf.n_first, me_first[h], pass_on)
    pl.when(z != zb)(lambda: bag_copy(z).wait_recv())
    gbias_r[...] = jnp.sum(bfin[1], 0)
    for h in range(2):
        hf = halves[h]
        chunks(0, hf.n_first, lambda p, h=h: cag_copy(h, p, 1 - core).wait_recv())
    grad_copies = [
        pltpu.make_async_copy(gall.at[k // 2, pl.ds((k % 2) * n_in, n_in)], gtaps_h.at[k] if k < 3 else gout_h, w_sem.at[2 + k])
        for k in range(4)
    ]
    for copy in grad_copies:
        copy.start()

    def sent(c):
        @pl.when(has_right)
        def _():
            act_right(c).wait_send()
            gp_right(c).wait_send()

        @pl.when(has_left)
        def _():
            act_left(c).wait_send()
            gp_left(c).wait_send()

        out_copy(c).wait()
        gsig_copy(c).wait()

    chunks(0, nc, sent)
    bias_core.wait_send()
    pl.when(z != zb)(lambda: b1_copy(z).wait_send())
    pl.when(z == zb)(lambda: ring(nz, z, lambda p: bag_copy(p).wait_send()))
    for h in range(2):
        hf = halves[h]
        core_copy(h).wait_send()

        def sent_first(p, h=h):
            s1_copy(h, p, me_first[h]).wait_send()
            ag1_copy(h, p, me_first[h]).wait_send()

        ring(hf.n_first, me_first[h], sent_first)
        chunks(0, hf.n_first, lambda p, h=h: cag_copy(h, p, core).wait_send())

        def sent_second(q, h=h, hf=hf):
            pl.when(q < hf.owners)(lambda: s2_copy(h, q, me_second[h]).wait_send())

        ring(hf.n_second, me_second[h], sent_second)

        @pl.when(me_second[h] < hf.owners)
        def _(h=h, hf=hf):
            ring(NX, x, lambda p: x_copy(h, p, x).wait_send())
            ring(hf.n_second, me_second[h], lambda p: ag2_copy(h, p, me_second[h]).wait_send())

    for copy in grad_copies:
        copy.wait()


def shards(sizes, signal, tap_weights, bias_inner, w_out, cotangent):
    n_seq, nyl = sizes
    nz, ny = n_seq // (2 * NYH * NX), NYH * nyl
    _, rows, c = signal.shape
    taps, _, hid = tap_weights.shape
    ch = CHUNK
    nc = rows // ch
    core_rows = (taps + 1) * c // 2
    share = SHARE * 8 // ny
    halves = (
        Half(0, share, ny, nz, 0),
        Half(share * ny, (core_rows - share * ny) // nz, nz, ny, 1),
    )
    cfg = (nz, ny, nyl, nc, ch, halves)
    any_spec = pl.BlockSpec(memory_space=pl.ANY)
    vmem_spec = pl.BlockSpec(memory_space=pltpu.VMEM)
    block = lambda dtype: pltpu.VMEM((nc, ch, c), dtype)
    dma = lambda *shape: pltpu.SemaphoreType.DMA(shape)
    most = max(ny, nz)
    ha, hb = halves
    scratch = [
        block(BF16), block(BF16), pltpu.VMEM(tap_weights.shape, BF16), pltpu.VMEM(w_out.shape, BF16),
        *[block(BF16)] * 8,
        block(F32), block(F32), block(F32),
        pltpu.VMEM((2, core_rows, hid), F32), pltpu.VMEM((8, hid), F32),
        pltpu.VMEM((core_rows, hid), BF16), pltpu.VMEM((core_rows, hid), BF16), pltpu.VMEM((8, hid), F32),
        *[pltpu.VMEM((h.n_first, h.piece, hid), BF16) for h in halves],
        *[pltpu.VMEM((h.n_first, h.piece, hid), BF16) for h in halves],
        pltpu.VMEM((nz, 8, hid), F32),
        *[pltpu.VMEM((h.owners * h.owned, hid), F32) for h in halves],
        *[pltpu.VMEM((h.n_second, h.owned, hid), F32) for h in halves],
        *[pltpu.VMEM((NX, h.owned, hid), F32) for h in halves],
        *[pltpu.VMEM((h.owners * h.owned, hid), F32) for h in halves],
        pltpu.VMEM((2, 8, hid), F32),
        pltpu.VMEM((2, core_rows, hid), BF16),
        dma(2 * nc), dma(6), dma(2 * nc),
        dma(2 * nc), dma(2 * nc), dma(2 * nc), dma(2 * nc),
        dma(3), dma(3), dma(2, most), dma(2, most), pltpu.SemaphoreType.DMA, dma(nz), dma(2, most), dma(2, most),
        dma(2, NX), dma(2, NX), dma(2, most), dma(2, most), dma(2, most), dma(2, most),
        dma(nz), pltpu.SemaphoreType.DMA, dma(2, most), dma(2, most),
    ]
    return pl.pallas_call(
        functools.partial(kernel, cfg),
        out_shape=(
            jax.ShapeDtypeStruct(signal.shape, BF16),
            jax.ShapeDtypeStruct(signal.shape, BF16),
            jax.ShapeDtypeStruct(tap_weights.shape, BF16),
            jax.ShapeDtypeStruct((hid,), F32),
            jax.ShapeDtypeStruct(w_out.shape, BF16),
        ),
        in_specs=[any_spec, any_spec, vmem_spec, any_spec, any_spec],
        out_specs=(any_spec, any_spec, any_spec, vmem_spec, any_spec),
        scratch_shapes=scratch,
        compiler_params=pltpu.CompilerParams(collective_id=0, has_side_effects=True, vmem_limit_bytes=48 * 1024 * 1024),
    )(signal, tap_weights, bias_inner, w_out, cotangent)


def solution(mesh):
    sizes = (mesh.shape["seq"], mesh.shape["grp"])
    return jax.shard_map(
        functools.partial(shards, sizes),
        mesh=mesh,
        in_specs=(P("grp", "seq", None), P(), P(), P(), P("grp", "seq", None)),
        out_specs=(P("grp", "seq", None), P("grp", "seq", None), P(), P(), P()),
        check_vma=False,
    )
```

```python
import functools
import math

import jax
import jax.numpy as jnp
from jax import lax
from jax.experimental import pallas as pl
from jax.experimental.pallas import tpu as pltpu
from jax.sharding import PartitionSpec as P

F32 = jnp.float32
BF16 = jnp.bfloat16
MESH = pl.DeviceIdType.MESH

NX = 4
NYH = 2
CHUNK = 128
SHARE = 64
STRAIGHT = 3, 6
CROSSING = 4, 8


def rows_dot(a, b):
    return lax.dot_general(a, b, (((1,), (0,)), ((), ())), preferred_element_type=F32)


def rows_dot_t(a, b):
    return lax.dot_general(a, b, (((1,), (1,)), ((), ())), preferred_element_type=F32)


def sum_rows_dot(a, b):
    return lax.dot_general(a, b, (((0,), (0,)), ((), ())), preferred_element_type=F32)


def cdf_of(v):
    return 0.5 * (1.0 + lax.erf(v * (1.0 / math.sqrt(2.0))))


def slope_of(v, cdf):
    return cdf + v * jnp.exp(-0.5 * v * v) * (1.0 / math.sqrt(2.0 * math.pi))


class Half:
    def __init__(self, start, piece, n_first, n_second):
        self.start, self.piece = start, piece
        self.n_first, self.n_second = n_first, n_second
        self.owners = max(n for n in range(1, NX + 1) if piece % (16 * n) == 0)
        self.owned = piece // self.owners


def kernel(cfg, *refs):
    nz, ny, nyl, nc, ch, halves = cfg
    (sig_h, taps_h, bias_r, wout_h, cot_h, out_h, gsig_h, grads_h, gbias_r,
     sig, cot, taps, wout, act, lead, trail, gp, gpl, gpr, hid, outb, gsb, pre, gh, slope,
     acc, bacc, cs, cr, bcr, s1s_a, s1s_b, s1r_a, s1r_b, b1r, bxr, bar, pp, xsb, xr_a, xr_b, ar_a, ar_b, bfin, gall,
     in_sem, w_sem, out_sem, act_s, act_r, gp_s, gp_r, c_s, c_r, s1_s, s1_r, b1_s, b1_r, bx_s, bx_r, bar_s, bar_r, bxg_s, bxg_r,
     x_s, x_r, ar_s, ar_r, xg_s, xg_r, ag1_s, ag1_r, bag_s, bag_r, cag_s, cag_r) = refs
    s1s, s1r, xr, ar = (s1s_a, s1s_b), (s1r_a, s1r_b), (xr_a, xr_b), (ar_a, ar_b)
    seq, grp = lax.axis_index("seq"), lax.axis_index("grp")
    hop = 2 * NYH
    core = seq % 2
    y = ((seq // 2) % NYH) * nyl + grp
    x = (seq // hop) % NX
    z = seq // (hop * NX)
    n_seq = nz * NX * hop
    has_right = seq + hop < n_seq
    has_left = seq >= hop
    right, left = (seq + hop, grp), (seq - hop, grp)
    other = (seq + 1 - 2 * core, grp)

    def y_peer(p):
        return (seq + (p // nyl - (seq // 2) % NYH) * 2, p % nyl)

    def z_peer(p):
        return (seq + (p - z) * (hop * NX), grp)

    def x_peer(p):
        return (seq + (p - x) * hop, grp)

    first, second = (y_peer, z_peer), (z_peer, y_peer)
    me_first, me_second = (y, z), (z, y)

    def remote(src, dst, send_sem, recv_sem, to):
        return pltpu.make_async_remote_copy(src_ref=src, dst_ref=dst, send_sem=send_sem, recv_sem=recv_sem,
                                            device_id=to, device_id_type=MESH)

    def ring(n, me, body):
        def step(k, carry):
            body(lax.rem(me + k, n))
            return carry
        lax.fori_loop(1, n, step, 0)

    def chunks(first_c, last_c, body):
        def step(c, carry):
            body(c)
            return carry
        lax.fori_loop(first_c, last_c, step, 0)

    barrier = pltpu.get_barrier_semaphore()

    def greet(to):
        pl.semaphore_signal(barrier, inc=1, device_id=to, device_id_type=MESH)

    cross_right = jnp.logical_and(x == NX - 1, has_right)
    cross_left = jnp.logical_and(x == 0, has_left)
    ring(NX, x, lambda p: greet(x_peer(p)))
    pl.when(cross_right)(lambda: greet(right))
    pl.when(cross_left)(lambda: greet(left))
    greet(other)
    ring(ny, y, lambda p: greet(y_peer(p)))
    ring(nz, z, lambda p: greet(z_peer(p)))
    greeted = 1 + (NX - 1) + (ny - 1) + (nz - 1)

    def sig_copy(c):
        return pltpu.make_async_copy(sig_h.at[0, pl.ds(pl.multiple_of(c * ch, ch), ch)], sig.at[c], in_sem.at[c])

    def cot_copy(c):
        return pltpu.make_async_copy(cot_h.at[0, pl.ds(pl.multiple_of(c * ch, ch), ch)], cot.at[c], in_sem.at[nc + c])

    taps_copy = pltpu.make_async_copy(taps_h, taps, w_sem.at[0])
    wout_copy = pltpu.make_async_copy(wout_h, wout, w_sem.at[1])
    chunks(0, nc, lambda c: sig_copy(c).start())
    taps_copy.start()
    wout_copy.start()
    chunks(0, nc, lambda c: cot_copy(c).start())

    def activate(c):
        sig_copy(c).wait()
        v = sig[c].astype(F32)
        act[c] = (v * cdf_of(v)).astype(BF16)

    def act_right(c):
        return remote(act.at[c], lead.at[c], act_s.at[c], act_r.at[c], right)

    def act_left(c):
        return remote(act.at[c], trail.at[c], act_s.at[nc + c], act_r.at[nc + c], left)

    def act_send(c):
        pl.when(has_right)(lambda: act_right(c).start())
        pl.when(has_left)(lambda: act_left(c).start())

    def gp_right(c):
        return remote(gp.at[c], gpl.at[c], gp_s.at[c], gp_r.at[c], right)

    def gp_left(c):
        return remote(gp.at[c], gpr.at[c], gp_s.at[nc + c], gp_r.at[nc + c], left)

    def gp_send(stage):
        for limits, crossing in ((STRAIGHT, False), (CROSSING, True)):
            ends = [0, *[min(n, nc - 1) for n in limits], nc]
            to_right = cross_right if crossing else jnp.logical_and(has_right, x != NX - 1)
            to_left = cross_left if crossing else jnp.logical_and(has_left, x != 0)
            pl.when(to_right)(lambda: chunks(ends[stage], ends[stage + 1], lambda c: gp_right(c).start()))
            pl.when(to_left)(lambda: chunks(ends[stage], ends[stage + 1], lambda c: gp_left(c).start()))

    activate(0)
    pl.semaphore_wait(barrier, greeted + jnp.where(cross_right, 1, 0) + jnp.where(cross_left, 1, 0))
    act_send(0)

    def activate_send(c):
        activate(c)
        act_send(c)

    chunks(1, nc, activate_send)

    @pl.when(jnp.logical_not(has_left))
    def _():
        lead[...] = jnp.zeros_like(lead)
        gpl[...] = jnp.zeros_like(gpl)

    @pl.when(jnp.logical_not(has_right))
    def _():
        trail[...] = jnp.zeros_like(trail)
        gpr[...] = jnp.zeros_like(gpr)

    acc[...] = jnp.zeros_like(acc)
    bacc[...] = jnp.zeros_like(bacc)
    bias = bias_r[...].reshape(1, -1)
    taps_copy.wait()
    wout_copy.wait()

    def prepare(c):
        cot_copy(c).wait()
        pre[c] = bias + rows_dot(act[c], taps[1])
        gh[c] = rows_dot_t(cot[c], wout[...])
        v = sig[c].astype(F32)
        slope[c] = slope_of(v, cdf_of(v))

    chunks(0, nc, prepare)

    def act_wait(c):
        pl.when(has_left)(lambda: act_right(c).wait_recv())
        pl.when(has_right)(lambda: act_left(c).wait_recv())

    def out_copy(c):
        return pltpu.make_async_copy(outb.at[c], out_h.at[0, pl.ds(pl.multiple_of(c * ch, ch), ch)], out_sem.at[c])

    def gsig_copy(c):
        return pltpu.make_async_copy(gsb.at[c], gsig_h.at[0, pl.ds(pl.multiple_of(c * ch, ch), ch)], out_sem.at[nc + c])

    n_in = taps.shape[1]

    def add_rows(k, value):
        acc[k // 2, pl.ds((k % 2) * n_in, n_in)] += value

    def work(c):
        lead_c, trail_c, act_c, cot_c = lead[c], trail[c], act[c], cot[c]
        v = pre[c] + rows_dot(lead_c, taps[0]) + rows_dot(trail_c, taps[2])
        cdf = cdf_of(v)
        hidden = (v * cdf).astype(BF16)
        grad = (gh[c] * slope_of(v, cdf)).astype(BF16)
        gp[c] = grad
        hid[c] = hidden
        add_rows(0, sum_rows_dot(lead_c, grad))
        add_rows(1, sum_rows_dot(act_c, grad))
        add_rows(2, sum_rows_dot(trail_c, grad))
        add_rows(3, sum_rows_dot(hidden, cot_c))
        wide = grad.astype(F32)
        bacc[...] += jnp.sum(wide.reshape(ch // 8, 8, wide.shape[-1]), 0)

    def project(c):
        outb[c] = (sig[c].astype(F32) + rows_dot(hid[c], wout[...])).astype(BF16)
        out_copy(c).start()

    def wait_work(c):
        act_wait(c)
        work(c)
        project(c)

    chunks(0, nc - 1, wait_work)
    act_wait(nc - 1)
    gp_send(0)
    work(nc - 1)

    def core_copy(h):
        rows = pl.ds(halves[h].start, halves[h].piece * halves[h].n_first)
        return remote(cs.at[rows], cr.at[rows], c_s.at[h], c_r.at[h], other)

    bias_core = remote(bacc, bcr, c_s.at[2], c_r.at[2], other)
    for h in range(2):
        rows = pl.ds(halves[h].start, halves[h].piece * halves[h].n_first)
        cs[rows] = acc[1 - core, rows].astype(BF16)
        core_copy(h).start()
    bias_core.start()
    project(nc - 1)

    zb = nz - 1

    def s1_copy(h, p, sender):
        return remote(s1s[h].at[p], s1r[h].at[sender], s1_s.at[h, p], s1_r.at[h, sender], first[h](p))

    def b1_copy(sender):
        return remote(bfin.at[0], b1r.at[sender], b1_s, b1_r.at[sender], z_peer(zb))

    for h in range(2):
        core_copy(h).wait_recv()
        hf = halves[h]

        def add_piece(p, h=h, hf=hf):
            rows = pl.ds(pl.multiple_of(hf.start + p * hf.piece, 16), hf.piece)
            total = acc[core, rows] + cr[rows].astype(F32)
            acc[core, rows] = total
            s1s[h][p] = total.astype(BF16)

        def add_send(p, h=h):
            add_piece(p)
            s1_copy(h, p, me_first[h]).start()

        ring(hf.n_first, me_first[h], add_send)
        add_piece(me_first[h])
    bias_core.wait_recv()
    bfin[0] = bacc[...] + bcr[...]
    pl.when(z != zb)(lambda: b1_copy(z).start())

    def adjoint(c):
        pl.when(has_left)(lambda: gp_right(c).wait_recv())
        pl.when(has_right)(lambda: gp_left(c).wait_recv())
        grad = rows_dot_t(gp[c], taps[1]) + rows_dot_t(gpr[c], taps[0]) + rows_dot_t(gpl[c], taps[2])
        gsb[c] = (cot[c].astype(F32) + grad * slope[c]).astype(BF16)
        gsig_copy(c).start()

    def slice_of(p, n):
        return pl.ds(pl.multiple_of(p * n, 16), n)

    xb = NX - 1

    def x_copy(h, p, sender):
        return remote(xsb.at[h, slice_of(p, halves[h].owned)], xr[h].at[sender], x_s.at[h, p], x_r.at[h, sender], x_peer(p))

    def bx_copy(sender):
        return remote(bfin.at[0], bxr.at[sender], bx_s, bx_r.at[sender], x_peer(xb))

    for h in range(2):
        hf = halves[h]
        rows = pl.ds(pl.multiple_of(hf.start + me_first[h] * hf.piece, 16), hf.piece)
        pp[h, pl.ds(0, hf.piece)] = acc[core, rows]

        def take(p, h=h, hf=hf):
            s1_copy(h, me_first[h], p).wait_recv()
            pp[h, pl.ds(0, hf.piece)] += s1r[h][p].astype(F32)

        ring(hf.n_first, me_first[h], take)
        xsb[h, pl.ds(0, hf.piece)] = pp[h, pl.ds(0, hf.piece)].astype(BF16)

        def scatter(p, h=h, hf=hf):
            pl.when(p < hf.owners)(lambda: x_copy(h, p, x).start())

        ring(NX, x, scatter)

    @pl.when(z == zb)
    def _():
        def take_bias(p):
            b1_copy(p).wait_recv()
            bfin[0] += b1r[p]

        ring(nz, z, take_bias)
        pl.when(x != xb)(lambda: bx_copy(x).start())

    gp_send(1)

    def ar_copy(h, p, sender):
        return remote(ar[h].at[sender], ar[h].at[sender], ar_s.at[h, p], ar_r.at[h, sender], second[h](p))

    def bar_copy(p, sender):
        return remote(bar.at[sender], bar.at[sender], bar_s.at[p], bar_r.at[sender], y_peer(p))

    for h in range(2):
        hf = halves[h]

        @pl.when(x < hf.owners)
        def _(h=h, hf=hf):
            rows = slice_of(x, hf.owned)

            def take(p):
                x_copy(h, x, p).wait_recv()
                pp[h, rows] += xr[h][p].astype(F32)

            ring(NX, x, take)
            ar[h][me_second[h]] = pp[h, rows].astype(BF16)
            ring(hf.n_second, me_second[h], lambda p: ar_copy(h, p, me_second[h]).start())

    owns_bias = jnp.logical_and(z == zb, x == xb)

    @pl.when(owns_bias)
    def _():
        def take_bias(p):
            bx_copy(p).wait_recv()
            bfin[0] += bxr[p]

        ring(NX, x, take_bias)
        bar[y] = bfin[0]
        ring(ny, y, lambda p: bar_copy(p, y).start())

    def piece_of(h, p):
        return pl.ds(pl.multiple_of(halves[h].start + p * halves[h].piece, 16), halves[h].piece)

    def xg_copy(h, p, sender):
        n = halves[h].owned
        start = halves[h].start + me_first[h] * halves[h].piece + sender * n
        ref = gall.at[core, pl.ds(pl.multiple_of(start, 16), n)]
        return remote(ref, ref, xg_s.at[h, p], xg_r.at[h, sender], x_peer(p))

    def bxg_copy(p):
        return remote(bfin.at[1], bfin.at[1], bxg_s.at[p], bxg_r, x_peer(p))

    for h in range(2):
        hf = halves[h]

        @pl.when(x < hf.owners)
        def _(h=h, hf=hf):
            ring(hf.n_second, me_second[h], lambda p: ar_copy(h, me_second[h], p).wait_recv())
            total = ar[h][0].astype(F32)
            for p in range(1, hf.n_second):
                total = total + ar[h][p].astype(F32)
            start = hf.start + me_first[h] * hf.piece + x * hf.owned
            gall[core, pl.ds(pl.multiple_of(start, 16), hf.owned)] = total.astype(BF16)
            ring(NX, x, lambda p: xg_copy(h, p, x).start())

    @pl.when(owns_bias)
    def _():
        ring(ny, y, lambda p: bar_copy(y, p).wait_recv())
        total = bar[0]
        for p in range(1, ny):
            total = total + bar[p]
        bfin[1] = total
        ring(NX, x, lambda p: bxg_copy(p).start())

    gp_send(2)

    def ag1_copy(h, p, sender):
        ref = gall.at[core, piece_of(h, sender)]
        return remote(ref, ref, ag1_s.at[h, p], ag1_r.at[h, sender], first[h](p))

    def cag_copy(h, p, side):
        ref = gall.at[side, piece_of(h, p)]
        return remote(ref, ref, cag_s.at[h, p], cag_r.at[h, p], other)

    def bag_copy(p):
        return remote(bfin.at[1], bfin.at[1], bag_s.at[p], bag_r, z_peer(p))

    for h in range(2):
        hf = halves[h]

        def take(p, h=h, hf=hf):
            pl.when(p < hf.owners)(lambda: xg_copy(h, x, p).wait_recv())

        ring(NX, x, take)
        ring(hf.n_first, me_first[h], lambda p, h=h: ag1_copy(h, p, me_first[h]).start())
        cag_copy(h, me_first[h], core).start()

    @pl.when(z == zb)
    def _():
        pl.when(x != xb)(lambda: bxg_copy(x).wait_recv())
        ring(nz, z, lambda p: bag_copy(p).start())

    chunks(0, nc, adjoint)

    for h in range(2):
        hf = halves[h]

        def pass_on(p, h=h):
            ag1_copy(h, me_first[h], p).wait_recv()
            cag_copy(h, p, core).start()

        ring(hf.n_first, me_first[h], pass_on)
    pl.when(z != zb)(lambda: bag_copy(z).wait_recv())
    gbias_r[...] = jnp.sum(bfin[1], 0)
    for h in range(2):
        hf = halves[h]
        chunks(0, hf.n_first, lambda p, h=h: cag_copy(h, p, 1 - core).wait_recv())
    grad_copy = pltpu.make_async_copy(gall, grads_h, w_sem.at[2])
    grad_copy.start()

    def sent(c):
        @pl.when(has_right)
        def _():
            act_right(c).wait_send()
            gp_right(c).wait_send()

        @pl.when(has_left)
        def _():
            act_left(c).wait_send()
            gp_left(c).wait_send()

        out_copy(c).wait()
        gsig_copy(c).wait()

    chunks(0, nc, sent)
    bias_core.wait_send()
    pl.when(z != zb)(lambda: b1_copy(z).wait_send())
    pl.when(z == zb)(lambda: ring(nz, z, lambda p: bag_copy(p).wait_send()))
    for h in range(2):
        hf = halves[h]
        core_copy(h).wait_send()

        def sent_first(p, h=h):
            s1_copy(h, p, me_first[h]).wait_send()
            ag1_copy(h, p, me_first[h]).wait_send()

        ring(hf.n_first, me_first[h], sent_first)
        chunks(0, hf.n_first, lambda p, h=h: cag_copy(h, p, core).wait_send())

        def sent_x(p, h=h, hf=hf):
            pl.when(p < hf.owners)(lambda: x_copy(h, p, x).wait_send())

        ring(NX, x, sent_x)

        @pl.when(x < hf.owners)
        def _(h=h, hf=hf):
            ring(NX, x, lambda p: xg_copy(h, p, x).wait_send())
            ring(hf.n_second, me_second[h], lambda p: ar_copy(h, p, me_second[h]).wait_send())

    pl.when(jnp.logical_and(z == zb, x != xb))(lambda: bx_copy(x).wait_send())

    @pl.when(owns_bias)
    def _():
        ring(ny, y, lambda p: bar_copy(p, y).wait_send())
        ring(NX, x, lambda p: bxg_copy(p).wait_send())

    grad_copy.wait()


def write_out(out_v, gsig_v, grads_v, gbias_v, out_h, gsig_h, gtaps_h, gbias_h, gout_h, sem):
    n_in = gtaps_h.shape[1]
    copies = [
        pltpu.make_async_copy(out_v, out_h, sem.at[0]),
        pltpu.make_async_copy(gsig_v, gsig_h, sem.at[1]),
        pltpu.make_async_copy(gbias_v, gbias_h, sem.at[2]),
    ]
    for k in range(4):
        part = grads_v.at[k // 2, pl.ds((k % 2) * n_in, n_in)]
        copies.append(pltpu.make_async_copy(part, gtaps_h.at[k] if k < 3 else gout_h, sem.at[3 + k]))
    for copy in copies:
        copy.start()
    for copy in copies:
        copy.wait()


def shards(sizes, signal, tap_weights, bias_inner, w_out, cotangent):
    n_seq, nyl = sizes
    nz, ny = n_seq // (2 * NYH * NX), NYH * nyl
    _, rows, c = signal.shape
    taps, _, hid = tap_weights.shape
    ch = CHUNK
    nc = rows // ch
    core_rows = (taps + 1) * c // 2
    share = SHARE * 8 // ny
    halves = (
        Half(0, share, ny, nz),
        Half(share * ny, (core_rows - share * ny) // nz, nz, ny),
    )
    cfg = (nz, ny, nyl, nc, ch, halves)
    any_spec = pl.BlockSpec(memory_space=pl.ANY)
    hbm_spec = pl.BlockSpec(memory_space=pltpu.HBM)
    vmem_spec = pl.BlockSpec(memory_space=pltpu.VMEM)
    block = lambda dtype: pltpu.VMEM((nc, ch, c), dtype)
    dma = lambda *shape: pltpu.SemaphoreType.DMA(shape)
    one = pltpu.SemaphoreType.DMA
    most = max(ny, nz)
    scratch = [
        block(BF16), block(BF16), pltpu.VMEM(tap_weights.shape, BF16), pltpu.VMEM(w_out.shape, BF16),
        *[block(BF16)] * 9,
        block(F32), block(F32), block(F32),
        pltpu.VMEM((2, core_rows, hid), F32), pltpu.VMEM((8, hid), F32),
        pltpu.VMEM((core_rows, hid), BF16), pltpu.VMEM((core_rows, hid), BF16), pltpu.VMEM((8, hid), F32),
        *[pltpu.VMEM((h.n_first, h.piece, hid), BF16) for h in halves],
        *[pltpu.VMEM((h.n_first, h.piece, hid), BF16) for h in halves],
        pltpu.VMEM((nz, 8, hid), F32),
        pltpu.VMEM((NX, 8, hid), F32), pltpu.VMEM((ny, 8, hid), F32),
        pltpu.VMEM((2, max(h.piece for h in halves), hid), F32), pltpu.VMEM((2, max(h.piece for h in halves), hid), BF16),
        *[pltpu.VMEM((NX, h.owned, hid), BF16) for h in halves],
        *[pltpu.VMEM((h.n_second, h.owned, hid), BF16) for h in halves],
        pltpu.VMEM((2, 8, hid), F32),
        pltpu.VMEM((2, core_rows, hid), BF16),
        dma(2 * nc), dma(6), dma(2 * nc),
        dma(2 * nc), dma(2 * nc), dma(2 * nc), dma(2 * nc),
        dma(3), dma(3), dma(2, most), dma(2, most), one, dma(nz), one, dma(NX), dma(ny), dma(ny), dma(NX), one,
        dma(2, NX), dma(2, NX), dma(2, most), dma(2, most), dma(2, NX), dma(2, NX), dma(2, most), dma(2, most),
        dma(nz), one, dma(2, most), dma(2, most),
    ]
    in_hbm = lambda value: pltpu.with_memory_space_constraint(value, pltpu.HBM)
    results = pl.pallas_call(
        functools.partial(kernel, cfg),
        out_shape=(
            pltpu.VMEM(signal.shape, BF16),
            pltpu.VMEM(signal.shape, BF16),
            pltpu.VMEM((2, core_rows, hid), BF16),
            pltpu.VMEM((hid,), F32),
        ),
        in_specs=[hbm_spec, hbm_spec, vmem_spec, hbm_spec, hbm_spec],
        out_specs=(any_spec, any_spec, any_spec, vmem_spec),
        scratch_shapes=scratch,
        compiler_params=pltpu.CompilerParams(collective_id=0, has_side_effects=True, vmem_limit_bytes=40 * 1024 * 1024),
    )(in_hbm(signal), in_hbm(tap_weights), in_hbm(bias_inner), in_hbm(w_out), in_hbm(cotangent))
    return pl.pallas_call(
        write_out,
        out_shape=(
            jax.ShapeDtypeStruct(signal.shape, BF16),
            jax.ShapeDtypeStruct(signal.shape, BF16),
            jax.ShapeDtypeStruct(tap_weights.shape, BF16),
            jax.ShapeDtypeStruct((hid,), F32),
            jax.ShapeDtypeStruct(w_out.shape, BF16),
        ),
        in_specs=[any_spec] * 4,
        out_specs=(hbm_spec,) * 5,
        scratch_shapes=[dma(7)],
        compiler_params=pltpu.CompilerParams(vmem_limit_bytes=8 * 1024 * 1024),
    )(*[pltpu.with_memory_space_constraint(value, pltpu.VMEM) for value in results])


def solution(mesh):
    sizes = (mesh.shape["seq"], mesh.shape["grp"])
    return jax.shard_map(
        functools.partial(shards, sizes),
        mesh=mesh,
        in_specs=(P("grp", "seq", None), P(), P(), P(), P("grp", "seq", None)),
        out_specs=(P("grp", "seq", None), P("grp", "seq", None), P(), P(), P()),
        check_vma=False,
    )
```

```python
import functools
import math

import jax
import jax.numpy as jnp
from jax import lax
from jax.experimental import pallas as pl
from jax.experimental.pallas import tpu as pltpu
from jax.sharding import PartitionSpec as P

F32 = jnp.float32
BF16 = jnp.bfloat16
MESH = pl.DeviceIdType.MESH

NX = 4
NYH = 2
CHUNK = 128
SHARE = 64
STRAIGHT = 3, 6
CROSSING = 4, 8


def rows_dot(a, b):
    return lax.dot_general(a, b, (((1,), (0,)), ((), ())), preferred_element_type=F32)


def rows_dot_t(a, b):
    return lax.dot_general(a, b, (((1,), (1,)), ((), ())), preferred_element_type=F32)


def sum_rows_dot(a, b):
    return lax.dot_general(a, b, (((0,), (0,)), ((), ())), preferred_element_type=F32)


def cdf_of(v):
    return 0.5 * (1.0 + lax.erf(v * (1.0 / math.sqrt(2.0))))


def slope_of(v, cdf):
    return cdf + v * jnp.exp(-0.5 * v * v) * (1.0 / math.sqrt(2.0 * math.pi))


class Half:
    def __init__(self, start, piece, n_first, n_second):
        self.start, self.piece = start, piece
        self.n_first, self.n_second = n_first, n_second
        self.owners = max(n for n in range(1, NX + 1) if piece % (16 * n) == 0)
        self.owned = piece // self.owners


def kernel(cfg, *refs):
    nz, ny, nyl, nc, ch, halves = cfg
    (sig_h, taps_h, bias_r, wout_h, cot_h, out_h, gsig_h, grads_h, gbias_r,
     sig, cot, taps, wout, act, lead, trail, gp, gpl, gpr, hid, outb, gsb, pre, gh, slope,
     acc, bacc, cs, cr, bcr, s1s_a, s1s_b, s1r_a, s1r_b, b1r, bxr, bar, pp, xsb, xr_a, xr_b, ar_a, ar_b, bfin, gall,
     in_sem, w_sem, out_sem, act_s, act_r, gp_s, gp_r, c_s, c_r, s1_s, s1_r, b1_s, b1_r, bx_s, bx_r, bar_s, bar_r, bxg_s, bxg_r,
     x_s, x_r, ar_s, ar_r, xg_s, xg_r, ag1_s, ag1_r, bag_s, bag_r, cag_s, cag_r) = refs
    s1s, s1r, xr, ar = (s1s_a, s1s_b), (s1r_a, s1r_b), (xr_a, xr_b), (ar_a, ar_b)
    seq, grp = lax.axis_index("seq"), lax.axis_index("grp")
    hop = 2 * NYH
    core = seq % 2
    y = ((seq // 2) % NYH) * nyl + grp
    x = (seq // hop) % NX
    z = seq // (hop * NX)
    n_seq = nz * NX * hop
    has_right = seq + hop < n_seq
    has_left = seq >= hop
    right, left = (seq + hop, grp), (seq - hop, grp)
    other = (seq + 1 - 2 * core, grp)

    def y_peer(p):
        return (seq + (p // nyl - (seq // 2) % NYH) * 2, p % nyl)

    def z_peer(p):
        return (seq + (p - z) * (hop * NX), grp)

    def x_peer(p):
        return (seq + (p - x) * hop, grp)

    first, second = (y_peer, z_peer), (z_peer, y_peer)
    me_first, me_second = (y, z), (z, y)

    def remote(src, dst, send_sem, recv_sem, to):
        return pltpu.make_async_remote_copy(src_ref=src, dst_ref=dst, send_sem=send_sem, recv_sem=recv_sem,
                                            device_id=to, device_id_type=MESH)

    def ring(n, me, body):
        def step(k, carry):
            body(lax.rem(me + k, n))
            return carry
        lax.fori_loop(1, n, step, 0, unroll=True)

    def chunks(first_c, last_c, body):
        def step(c, carry):
            body(c)
            return carry
        lax.fori_loop(first_c, last_c, step, 0)

    barrier = pltpu.get_barrier_semaphore()

    def greet(to):
        pl.semaphore_signal(barrier, inc=1, device_id=to, device_id_type=MESH)

    cross_right = jnp.logical_and(x == NX - 1, has_right)
    cross_left = jnp.logical_and(x == 0, has_left)
    ring(NX, x, lambda p: greet(x_peer(p)))
    pl.when(cross_right)(lambda: greet(right))
    pl.when(cross_left)(lambda: greet(left))
    greet(other)
    ring(ny, y, lambda p: greet(y_peer(p)))
    ring(nz, z, lambda p: greet(z_peer(p)))
    greeted = 1 + (NX - 1) + (ny - 1) + (nz - 1)

    def sig_copy(c):
        return pltpu.make_async_copy(sig_h.at[0, pl.ds(pl.multiple_of(c * ch, ch), ch)], sig.at[c], in_sem.at[c])

    def cot_copy(c):
        return pltpu.make_async_copy(cot_h.at[0, pl.ds(pl.multiple_of(c * ch, ch), ch)], cot.at[c], in_sem.at[nc + c])

    taps_copy = pltpu.make_async_copy(taps_h, taps, w_sem.at[0])
    wout_copy = pltpu.make_async_copy(wout_h, wout, w_sem.at[1])
    chunks(0, nc, lambda c: sig_copy(c).start())
    taps_copy.start()
    wout_copy.start()
    chunks(0, nc, lambda c: cot_copy(c).start())

    def activate(c):
        sig_copy(c).wait()
        v = sig[c].astype(F32)
        act[c] = (v * cdf_of(v)).astype(BF16)

    def act_right(c):
        return remote(act.at[c], lead.at[c], act_s.at[c], act_r.at[c], right)

    def act_left(c):
        return remote(act.at[c], trail.at[c], act_s.at[nc + c], act_r.at[nc + c], left)

    def act_send(c):
        pl.when(has_right)(lambda: act_right(c).start())
        pl.when(has_left)(lambda: act_left(c).start())

    def gp_right(c):
        return remote(gp.at[c], gpl.at[c], gp_s.at[c], gp_r.at[c], right)

    def gp_left(c):
        return remote(gp.at[c], gpr.at[c], gp_s.at[nc + c], gp_r.at[nc + c], left)

    def gp_send(stage):
        for limits, crossing in ((STRAIGHT, False), (CROSSING, True)):
            ends = [0, *[min(n, nc - 1) for n in limits], nc]
            to_right = cross_right if crossing else jnp.logical_and(has_right, x != NX - 1)
            to_left = cross_left if crossing else jnp.logical_and(has_left, x != 0)
            pl.when(to_right)(lambda: chunks(ends[stage], ends[stage + 1], lambda c: gp_right(c).start()))
            pl.when(to_left)(lambda: chunks(ends[stage], ends[stage + 1], lambda c: gp_left(c).start()))

    activate(0)
    pl.semaphore_wait(barrier, greeted + jnp.where(cross_right, 1, 0) + jnp.where(cross_left, 1, 0))
    act_send(0)

    def activate_send(c):
        activate(c)
        act_send(c)

    chunks(1, nc, activate_send)

    @pl.when(jnp.logical_not(has_left))
    def _():
        lead[...] = jnp.zeros_like(lead)
        gpl[...] = jnp.zeros_like(gpl)

    @pl.when(jnp.logical_not(has_right))
    def _():
        trail[...] = jnp.zeros_like(trail)
        gpr[...] = jnp.zeros_like(gpr)

    acc[...] = jnp.zeros_like(acc)
    bacc[...] = jnp.zeros_like(bacc)
    bias = bias_r[...].reshape(1, -1)
    taps_copy.wait()
    wout_copy.wait()

    def prepare(c):
        cot_copy(c).wait()
        pre[c] = bias + rows_dot(act[c], taps[1])
        gh[c] = rows_dot_t(cot[c], wout[...])
        v = sig[c].astype(F32)
        slope[c] = slope_of(v, cdf_of(v))

    chunks(0, nc, prepare)

    def act_wait(c):
        pl.when(has_left)(lambda: act_right(c).wait_recv())
        pl.when(has_right)(lambda: act_left(c).wait_recv())

    def out_copy(c):
        return pltpu.make_async_copy(outb.at[c], out_h.at[0, pl.ds(pl.multiple_of(c * ch, ch), ch)], out_sem.at[c])

    def gsig_copy(c):
        return pltpu.make_async_copy(gsb.at[c], gsig_h.at[0, pl.ds(pl.multiple_of(c * ch, ch), ch)], out_sem.at[nc + c])

    n_in = taps.shape[1]

    def add_rows(k, value):
        acc[k // 2, pl.ds((k % 2) * n_in, n_in)] += value

    def work(c):
        lead_c, trail_c, act_c, cot_c = lead[c], trail[c], act[c], cot[c]
        v = pre[c] + rows_dot(lead_c, taps[0]) + rows_dot(trail_c, taps[2])
        cdf = cdf_of(v)
        hidden = (v * cdf).astype(BF16)
        grad = (gh[c] * slope_of(v, cdf)).astype(BF16)
        gp[c] = grad
        hid[c] = hidden
        add_rows(0, sum_rows_dot(lead_c, grad))
        add_rows(1, sum_rows_dot(act_c, grad))
        add_rows(2, sum_rows_dot(trail_c, grad))
        add_rows(3, sum_rows_dot(hidden, cot_c))
        wide = grad.astype(F32)
        bacc[...] += jnp.sum(wide.reshape(ch // 8, 8, wide.shape[-1]), 0)

    def project(c):
        outb[c] = (sig[c].astype(F32) + rows_dot(hid[c], wout[...])).astype(BF16)
        out_copy(c).start()

    def wait_work(c):
        act_wait(c)
        work(c)
        project(c)

    chunks(0, nc - 1, wait_work)
    act_wait(nc - 1)
    gp_send(0)
    work(nc - 1)

    def core_copy(h):
        rows = pl.ds(halves[h].start, halves[h].piece * halves[h].n_first)
        return remote(cs.at[rows], cr.at[rows], c_s.at[h], c_r.at[h], other)

    bias_core = remote(bacc, bcr, c_s.at[2], c_r.at[2], other)
    for h in range(2):
        rows = pl.ds(halves[h].start, halves[h].piece * halves[h].n_first)
        cs[rows] = acc[1 - core, rows].astype(BF16)
        core_copy(h).start()
    bias_core.start()
    project(nc - 1)

    zb = nz - 1

    def s1_copy(h, p, sender):
        return remote(s1s[h].at[p], s1r[h].at[sender], s1_s.at[h, p], s1_r.at[h, sender], first[h](p))

    def b1_copy(sender):
        return remote(bfin.at[0], b1r.at[sender], b1_s, b1_r.at[sender], z_peer(zb))

    for h in range(2):
        core_copy(h).wait_recv()
        hf = halves[h]

        def add_piece(p, h=h, hf=hf):
            rows = pl.ds(pl.multiple_of(hf.start + p * hf.piece, 16), hf.piece)
            total = acc[core, rows] + cr[rows].astype(F32)
            acc[core, rows] = total
            s1s[h][p] = total.astype(BF16)

        def add_send(p, h=h):
            add_piece(p)
            s1_copy(h, p, me_first[h]).start()

        ring(hf.n_first, me_first[h], add_send)
        add_piece(me_first[h])
    bias_core.wait_recv()
    bfin[0] = bacc[...] + bcr[...]
    pl.when(z != zb)(lambda: b1_copy(z).start())

    def adjoint(c):
        pl.when(has_left)(lambda: gp_right(c).wait_recv())
        pl.when(has_right)(lambda: gp_left(c).wait_recv())
        grad = rows_dot_t(gp[c], taps[1]) + rows_dot_t(gpr[c], taps[0]) + rows_dot_t(gpl[c], taps[2])
        gsb[c] = (cot[c].astype(F32) + grad * slope[c]).astype(BF16)
        gsig_copy(c).start()

    def slice_of(p, n):
        return pl.ds(pl.multiple_of(p * n, 16), n)

    xb = NX - 1

    def x_copy(h, p, sender):
        return remote(xsb.at[h, slice_of(p, halves[h].owned)], xr[h].at[sender], x_s.at[h, p], x_r.at[h, sender], x_peer(p))

    def bx_copy(sender):
        return remote(bfin.at[0], bxr.at[sender], bx_s, bx_r.at[sender], x_peer(xb))

    for h in range(2):
        hf = halves[h]
        rows = pl.ds(pl.multiple_of(hf.start + me_first[h] * hf.piece, 16), hf.piece)
        pp[h, pl.ds(0, hf.piece)] = acc[core, rows]

        def take(p, h=h, hf=hf):
            s1_copy(h, me_first[h], p).wait_recv()
            pp[h, pl.ds(0, hf.piece)] += s1r[h][p].astype(F32)

        ring(hf.n_first, me_first[h], take)
        xsb[h, pl.ds(0, hf.piece)] = pp[h, pl.ds(0, hf.piece)].astype(BF16)

        def scatter(p, h=h, hf=hf):
            pl.when(p < hf.owners)(lambda: x_copy(h, p, x).start())

        ring(NX, x, scatter)

    @pl.when(z == zb)
    def _():
        def take_bias(p):
            b1_copy(p).wait_recv()
            bfin[0] += b1r[p]

        ring(nz, z, take_bias)
        pl.when(x != xb)(lambda: bx_copy(x).start())

    gp_send(1)

    def ar_copy(h, p, sender):
        return remote(ar[h].at[sender], ar[h].at[sender], ar_s.at[h, p], ar_r.at[h, sender], second[h](p))

    def bar_copy(p, sender):
        return remote(bar.at[sender], bar.at[sender], bar_s.at[p], bar_r.at[sender], y_peer(p))

    for h in range(2):
        hf = halves[h]

        @pl.when(x < hf.owners)
        def _(h=h, hf=hf):
            rows = slice_of(x, hf.owned)

            def take(p):
                x_copy(h, x, p).wait_recv()
                pp[h, rows] += xr[h][p].astype(F32)

            ring(NX, x, take)
            ar[h][me_second[h]] = pp[h, rows].astype(BF16)
            ring(hf.n_second, me_second[h], lambda p: ar_copy(h, p, me_second[h]).start())

    owns_bias = jnp.logical_and(z == zb, x == xb)

    @pl.when(owns_bias)
    def _():
        def take_bias(p):
            bx_copy(p).wait_recv()
            bfin[0] += bxr[p]

        ring(NX, x, take_bias)
        bar[y] = bfin[0]
        ring(ny, y, lambda p: bar_copy(p, y).start())

    def piece_of(h, p):
        return pl.ds(pl.multiple_of(halves[h].start + p * halves[h].piece, 16), halves[h].piece)

    def xg_copy(h, p, sender):
        n = halves[h].owned
        start = halves[h].start + me_first[h] * halves[h].piece + sender * n
        ref = gall.at[core, pl.ds(pl.multiple_of(start, 16), n)]
        return remote(ref, ref, xg_s.at[h, p], xg_r.at[h, sender], x_peer(p))

    def bxg_copy(p):
        return remote(bfin.at[1], bfin.at[1], bxg_s.at[p], bxg_r, x_peer(p))

    for h in range(2):
        hf = halves[h]

        @pl.when(x < hf.owners)
        def _(h=h, hf=hf):
            ring(hf.n_second, me_second[h], lambda p: ar_copy(h, me_second[h], p).wait_recv())
            total = ar[h][0].astype(F32)
            for p in range(1, hf.n_second):
                total = total + ar[h][p].astype(F32)
            start = hf.start + me_first[h] * hf.piece + x * hf.owned
            gall[core, pl.ds(pl.multiple_of(start, 16), hf.owned)] = total.astype(BF16)
            ring(NX, x, lambda p: xg_copy(h, p, x).start())

    @pl.when(owns_bias)
    def _():
        ring(ny, y, lambda p: bar_copy(y, p).wait_recv())
        total = bar[0]
        for p in range(1, ny):
            total = total + bar[p]
        bfin[1] = total
        ring(NX, x, lambda p: bxg_copy(p).start())

    gp_send(2)

    def ag1_copy(h, p, sender):
        ref = gall.at[core, piece_of(h, sender)]
        return remote(ref, ref, ag1_s.at[h, p], ag1_r.at[h, sender], first[h](p))

    def cag_copy(h, p, side):
        ref = gall.at[side, piece_of(h, p)]
        return remote(ref, ref, cag_s.at[h, p], cag_r.at[h, p], other)

    def bag_copy(p):
        return remote(bfin.at[1], bfin.at[1], bag_s.at[p], bag_r, z_peer(p))

    for h in range(2):
        hf = halves[h]

        def take(p, h=h, hf=hf):
            pl.when(p < hf.owners)(lambda: xg_copy(h, x, p).wait_recv())

        ring(NX, x, take)
        ring(hf.n_first, me_first[h], lambda p, h=h: ag1_copy(h, p, me_first[h]).start())
        cag_copy(h, me_first[h], core).start()

    @pl.when(z == zb)
    def _():
        pl.when(x != xb)(lambda: bxg_copy(x).wait_recv())
        ring(nz, z, lambda p: bag_copy(p).start())

    chunks(0, nc - 2, adjoint)

    for h in range(2):
        hf = halves[h]

        def pass_on(p, h=h):
            ag1_copy(h, me_first[h], p).wait_recv()
            cag_copy(h, p, core).start()

        ring(hf.n_first, me_first[h], pass_on)
    def grad_copy(side):
        return pltpu.make_async_copy(gall.at[side], grads_h.at[side], w_sem.at[2 + side])

    grad_copy(core).start()
    chunks(nc - 2, nc, adjoint)
    pl.when(z != zb)(lambda: bag_copy(z).wait_recv())
    gbias_r[...] = jnp.sum(bfin[1], 0)
    for h in range(2):
        hf = halves[h]
        chunks(0, hf.n_first, lambda p, h=h: cag_copy(h, p, 1 - core).wait_recv())
    grad_copy(1 - core).start()

    def sent(c):
        @pl.when(has_right)
        def _():
            act_right(c).wait_send()
            gp_right(c).wait_send()

        @pl.when(has_left)
        def _():
            act_left(c).wait_send()
            gp_left(c).wait_send()

        out_copy(c).wait()
        gsig_copy(c).wait()

    chunks(0, nc, sent)
    bias_core.wait_send()
    pl.when(z != zb)(lambda: b1_copy(z).wait_send())
    pl.when(z == zb)(lambda: ring(nz, z, lambda p: bag_copy(p).wait_send()))
    for h in range(2):
        hf = halves[h]
        core_copy(h).wait_send()

        def sent_first(p, h=h):
            s1_copy(h, p, me_first[h]).wait_send()
            ag1_copy(h, p, me_first[h]).wait_send()

        ring(hf.n_first, me_first[h], sent_first)
        chunks(0, hf.n_first, lambda p, h=h: cag_copy(h, p, core).wait_send())

        def sent_x(p, h=h, hf=hf):
            pl.when(p < hf.owners)(lambda: x_copy(h, p, x).wait_send())

        ring(NX, x, sent_x)

        @pl.when(x < hf.owners)
        def _(h=h, hf=hf):
            ring(NX, x, lambda p: xg_copy(h, p, x).wait_send())
            ring(hf.n_second, me_second[h], lambda p: ar_copy(h, p, me_second[h]).wait_send())

    pl.when(jnp.logical_and(z == zb, x != xb))(lambda: bx_copy(x).wait_send())

    @pl.when(owns_bias)
    def _():
        ring(ny, y, lambda p: bar_copy(p, y).wait_send())
        ring(NX, x, lambda p: bxg_copy(p).wait_send())

    grad_copy(0).wait()
    grad_copy(1).wait()


def write_out(out_v, gsig_v, grads_v, gbias_v, out_h, gsig_h, gtaps_h, gbias_h, gout_h, sem):
    n_in = gtaps_h.shape[1]
    copies = [
        pltpu.make_async_copy(out_v, out_h, sem.at[0]),
        pltpu.make_async_copy(gsig_v, gsig_h, sem.at[1]),
        pltpu.make_async_copy(gbias_v, gbias_h, sem.at[2]),
    ]
    for k in range(4):
        part = grads_v.at[k // 2, pl.ds((k % 2) * n_in, n_in)]
        copies.append(pltpu.make_async_copy(part, gtaps_h.at[k] if k < 3 else gout_h, sem.at[3 + k]))
    for copy in copies:
        copy.start()
    for copy in copies:
        copy.wait()


def shards(sizes, signal, tap_weights, bias_inner, w_out, cotangent):
    n_seq, nyl = sizes
    nz, ny = n_seq // (2 * NYH * NX), NYH * nyl
    _, rows, c = signal.shape
    taps, _, hid = tap_weights.shape
    ch = CHUNK
    nc = rows // ch
    core_rows = (taps + 1) * c // 2
    share = SHARE * 8 // ny
    halves = (
        Half(0, share, ny, nz),
        Half(share * ny, (core_rows - share * ny) // nz, nz, ny),
    )
    cfg = (nz, ny, nyl, nc, ch, halves)
    any_spec = pl.BlockSpec(memory_space=pl.ANY)
    hbm_spec = pl.BlockSpec(memory_space=pltpu.HBM)
    vmem_spec = pl.BlockSpec(memory_space=pltpu.VMEM)
    block = lambda dtype: pltpu.VMEM((nc, ch, c), dtype)
    dma = lambda *shape: pltpu.SemaphoreType.DMA(shape)
    one = pltpu.SemaphoreType.DMA
    most = max(ny, nz)
    scratch = [
        block(BF16), block(BF16), pltpu.VMEM(tap_weights.shape, BF16), pltpu.VMEM(w_out.shape, BF16),
        *[block(BF16)] * 9,
        block(F32), block(F32), block(F32),
        pltpu.VMEM((2, core_rows, hid), F32), pltpu.VMEM((8, hid), F32),
        pltpu.VMEM((core_rows, hid), BF16), pltpu.VMEM((core_rows, hid), BF16), pltpu.VMEM((8, hid), F32),
        *[pltpu.VMEM((h.n_first, h.piece, hid), BF16) for h in halves],
        *[pltpu.VMEM((h.n_first, h.piece, hid), BF16) for h in halves],
        pltpu.VMEM((nz, 8, hid), F32),
        pltpu.VMEM((NX, 8, hid), F32), pltpu.VMEM((ny, 8, hid), F32),
        pltpu.VMEM((2, max(h.piece for h in halves), hid), F32), pltpu.VMEM((2, max(h.piece for h in halves), hid), BF16),
        *[pltpu.VMEM((NX, h.owned, hid), BF16) for h in halves],
        *[pltpu.VMEM((h.n_second, h.owned, hid), BF16) for h in halves],
        pltpu.VMEM((2, 8, hid), F32),
        pltpu.VMEM((2, core_rows, hid), BF16),
        dma(2 * nc), dma(6), dma(2 * nc),
        dma(2 * nc), dma(2 * nc), dma(2 * nc), dma(2 * nc),
        dma(3), dma(3), dma(2, most), dma(2, most), one, dma(nz), one, dma(NX), dma(ny), dma(ny), dma(NX), one,
        dma(2, NX), dma(2, NX), dma(2, most), dma(2, most), dma(2, NX), dma(2, NX), dma(2, most), dma(2, most),
        dma(nz), one, dma(2, most), dma(2, most),
    ]
    in_hbm = lambda value: pltpu.with_memory_space_constraint(value, pltpu.HBM)
    results = pl.pallas_call(
        functools.partial(kernel, cfg),
        out_shape=(
            pltpu.VMEM(signal.shape, BF16),
            pltpu.VMEM(signal.shape, BF16),
            pltpu.VMEM((2, core_rows, hid), BF16),
            pltpu.VMEM((hid,), F32),
        ),
        in_specs=[hbm_spec, hbm_spec, vmem_spec, hbm_spec, hbm_spec],
        out_specs=(any_spec, any_spec, any_spec, vmem_spec),
        scratch_shapes=scratch,
        compiler_params=pltpu.CompilerParams(collective_id=0, has_side_effects=True, vmem_limit_bytes=40 * 1024 * 1024),
    )(in_hbm(signal), in_hbm(tap_weights), in_hbm(bias_inner), in_hbm(w_out), in_hbm(cotangent))
    return pl.pallas_call(
        write_out,
        out_shape=(
            jax.ShapeDtypeStruct(signal.shape, BF16),
            jax.ShapeDtypeStruct(signal.shape, BF16),
            jax.ShapeDtypeStruct(tap_weights.shape, BF16),
            jax.ShapeDtypeStruct((hid,), F32),
            jax.ShapeDtypeStruct(w_out.shape, BF16),
        ),
        in_specs=[any_spec] * 4,
        out_specs=(hbm_spec,) * 5,
        scratch_shapes=[dma(7)],
        compiler_params=pltpu.CompilerParams(vmem_limit_bytes=8 * 1024 * 1024),
    )(*[pltpu.with_memory_space_constraint(value, pltpu.VMEM) for value in results])


def solution(mesh):
    sizes = (mesh.shape["seq"], mesh.shape["grp"])
    return jax.shard_map(
        functools.partial(shards, sizes),
        mesh=mesh,
        in_specs=(P("grp", "seq", None), P(), P(), P(), P("grp", "seq", None)),
        out_specs=(P("grp", "seq", None), P("grp", "seq", None), P(), P(), P()),
        check_vma=False,
    )
```

```python
import functools
import math

import jax
import jax.numpy as jnp
from jax import lax
from jax.experimental import pallas as pl
from jax.experimental.pallas import tpu as pltpu
from jax.sharding import PartitionSpec as P

F32 = jnp.float32
BF16 = jnp.bfloat16
MESH = pl.DeviceIdType.MESH

NX = 4
NYH = 2
CHUNK = 128
SHARE = 32
STRAIGHT = 2, 3, 6
CROSSING = 2, 3, 6


def rows_dot(a, b):
    return lax.dot_general(a, b, (((1,), (0,)), ((), ())), preferred_element_type=F32)


def rows_dot_t(a, b):
    return lax.dot_general(a, b, (((1,), (1,)), ((), ())), preferred_element_type=F32)


def sum_rows_dot(a, b):
    return lax.dot_general(a, b, (((0,), (0,)), ((), ())), preferred_element_type=F32)


def cdf_of(v):
    return 0.5 * (1.0 + lax.erf(v * (1.0 / math.sqrt(2.0))))


def slope_of(v, cdf):
    return cdf + v * jnp.exp(-0.5 * v * v) * (1.0 / math.sqrt(2.0 * math.pi))


class Half:
    def __init__(self, start, piece, n_first, n_middle, n_last):
        self.start, self.piece = start, piece
        self.n_first, self.n_middle, self.n_last = n_first, n_middle, n_last
        self.owners = max(n for n in range(1, n_middle + 1) if piece % (16 * n) == 0)
        self.owned = piece // self.owners


def kernel(cfg, *refs):
    nz, ny, nyl, nc, ch, halves = cfg
    (sig_h, taps_h, bias_r, wout_h, cot_h, out_h, gsig_h, grads_h, gbias_r,
     sig, cot, taps, wout, act, lead, trail, gp, gpl, gpr, hid, outb, gsb, pre, gh, slope,
     acc, bacc, cs, cr, bcr, s1s_a, s1s_b, s1r_a, s1r_b, b1r, bxr, bar, pp, xsb, xr_a, xr_b, ar_a, ar_b, bfin, gall,
     in_sem, w_sem, out_sem, act_s, act_r, gp_s, gp_r, c_s, c_r, s1_s, s1_r, b1_s, b1_r, bx_s, bx_r, bar_s, bar_r, bxg_s, bxg_r,
     x_s, x_r, ar_s, ar_r, xg_s, xg_r, ag1_s, ag1_r, bag_s, bag_r, cag_s, cag_r) = refs
    s1s, s1r, xr, ar = (s1s_a, s1s_b), (s1r_a, s1r_b), (xr_a, xr_b), (ar_a, ar_b)
    seq, grp = lax.axis_index("seq"), lax.axis_index("grp")
    hop = 2 * NYH
    core = seq % 2
    y = ((seq // 2) % NYH) * nyl + grp
    x = (seq // hop) % NX
    z = seq // (hop * NX)
    n_seq = nz * NX * hop
    has_right = seq + hop < n_seq
    has_left = seq >= hop
    right, left = (seq + hop, grp), (seq - hop, grp)
    other = (seq + 1 - 2 * core, grp)

    def y_peer(p):
        return (seq + (p // nyl - (seq // 2) % NYH) * 2, p % nyl)

    def z_peer(p):
        return (seq + (p - z) * (hop * NX), grp)

    def x_peer(p):
        return (seq + (p - x) * hop, grp)

    first, middle, last = (y_peer, x_peer), (x_peer, y_peer), (z_peer, z_peer)
    me_first, me_middle, me_last = (y, x), (x, y), (z, z)

    def remote(src, dst, send_sem, recv_sem, to):
        return pltpu.make_async_remote_copy(src_ref=src, dst_ref=dst, send_sem=send_sem, recv_sem=recv_sem,
                                            device_id=to, device_id_type=MESH)

    def ring(n, me, body):
        def step(k, carry):
            body(lax.rem(me + k, n))
            return carry
        lax.fori_loop(1, n, step, 0, unroll=True)

    def chunks(first_c, last_c, body):
        def step(c, carry):
            body(c)
            return carry
        lax.fori_loop(first_c, last_c, step, 0)

    barrier = pltpu.get_barrier_semaphore()

    def greet(to):
        pl.semaphore_signal(barrier, inc=1, device_id=to, device_id_type=MESH)

    cross_right = jnp.logical_and(x == NX - 1, has_right)
    cross_left = jnp.logical_and(x == 0, has_left)
    ring(NX, x, lambda p: greet(x_peer(p)))
    pl.when(cross_right)(lambda: greet(right))
    pl.when(cross_left)(lambda: greet(left))
    greet(other)
    ring(ny, y, lambda p: greet(y_peer(p)))
    ring(nz, z, lambda p: greet(z_peer(p)))
    greeted = 1 + (NX - 1) + (ny - 1) + (nz - 1)

    def sig_copy(c):
        return pltpu.make_async_copy(sig_h.at[0, pl.ds(pl.multiple_of(c * ch, ch), ch)], sig.at[c], in_sem.at[c])

    def cot_copy(c):
        return pltpu.make_async_copy(cot_h.at[0, pl.ds(pl.multiple_of(c * ch, ch), ch)], cot.at[c], in_sem.at[nc + c])

    taps_copy = pltpu.make_async_copy(taps_h, taps, w_sem.at[0])
    wout_copy = pltpu.make_async_copy(wout_h, wout, w_sem.at[1])
    chunks(0, nc, lambda c: sig_copy(c).start())
    taps_copy.start()
    wout_copy.start()
    chunks(0, nc, lambda c: cot_copy(c).start())

    def activate(c):
        sig_copy(c).wait()
        v = sig[c].astype(F32)
        act[c] = (v * cdf_of(v)).astype(BF16)

    def act_right(c):
        return remote(act.at[c], lead.at[c], act_s.at[c], act_r.at[c], right)

    def act_left(c):
        return remote(act.at[c], trail.at[c], act_s.at[nc + c], act_r.at[nc + c], left)

    def act_send(c):
        pl.when(has_right)(lambda: act_right(c).start())
        pl.when(has_left)(lambda: act_left(c).start())

    def gp_right(c):
        return remote(gp.at[c], gpl.at[c], gp_s.at[c], gp_r.at[c], right)

    def gp_left(c):
        return remote(gp.at[c], gpr.at[c], gp_s.at[nc + c], gp_r.at[nc + c], left)

    def gp_send(stage):
        for limits, crossing in ((STRAIGHT, False), (CROSSING, True)):
            ends = [0, min(limits[0], nc - 1), *[min(n, nc) for n in limits[1:]], nc]
            to_right = cross_right if crossing else jnp.logical_and(has_right, x != NX - 1)
            to_left = cross_left if crossing else jnp.logical_and(has_left, x != 0)
            pl.when(to_right)(lambda: chunks(ends[stage], ends[stage + 1], lambda c: gp_right(c).start()))
            pl.when(to_left)(lambda: chunks(ends[stage], ends[stage + 1], lambda c: gp_left(c).start()))

    activate(0)
    pl.semaphore_wait(barrier, greeted + jnp.where(cross_right, 1, 0) + jnp.where(cross_left, 1, 0))
    act_send(0)

    def activate_send(c):
        activate(c)
        act_send(c)

    chunks(1, nc, activate_send)

    @pl.when(jnp.logical_not(has_left))
    def _():
        lead[...] = jnp.zeros_like(lead)
        gpl[...] = jnp.zeros_like(gpl)

    @pl.when(jnp.logical_not(has_right))
    def _():
        trail[...] = jnp.zeros_like(trail)
        gpr[...] = jnp.zeros_like(gpr)

    acc[...] = jnp.zeros_like(acc)
    bacc[...] = jnp.zeros_like(bacc)
    bias = bias_r[...].reshape(1, -1)
    taps_copy.wait()
    wout_copy.wait()

    def prepare(c):
        cot_copy(c).wait()
        pre[c] = bias + rows_dot(act[c], taps[1])
        gh[c] = rows_dot_t(cot[c], wout[...])
        v = sig[c].astype(F32)
        slope[c] = slope_of(v, cdf_of(v))

    chunks(0, nc, prepare)

    def act_wait(c):
        pl.when(has_left)(lambda: act_right(c).wait_recv())
        pl.when(has_right)(lambda: act_left(c).wait_recv())

    def out_copy(c):
        return pltpu.make_async_copy(outb.at[c], out_h.at[0, pl.ds(pl.multiple_of(c * ch, ch), ch)], out_sem.at[c])

    def gsig_copy(c):
        return pltpu.make_async_copy(gsb.at[c], gsig_h.at[0, pl.ds(pl.multiple_of(c * ch, ch), ch)], out_sem.at[nc + c])

    n_in = taps.shape[1]

    def add_rows(k, value):
        acc[k // 2, pl.ds((k % 2) * n_in, n_in)] += value

    def work(c):
        lead_c, trail_c, act_c, cot_c = lead[c], trail[c], act[c], cot[c]
        v = pre[c] + rows_dot(lead_c, taps[0]) + rows_dot(trail_c, taps[2])
        cdf = cdf_of(v)
        hidden = (v * cdf).astype(BF16)
        grad = (gh[c] * slope_of(v, cdf)).astype(BF16)
        gp[c] = grad
        hid[c] = hidden
        add_rows(0, sum_rows_dot(lead_c, grad))
        add_rows(1, sum_rows_dot(act_c, grad))
        add_rows(2, sum_rows_dot(trail_c, grad))
        add_rows(3, sum_rows_dot(hidden, cot_c))
        wide = grad.astype(F32)
        bacc[...] += jnp.sum(wide.reshape(ch // 8, 8, wide.shape[-1]), 0)

    def project(c):
        outb[c] = (sig[c].astype(F32) + rows_dot(hid[c], wout[...])).astype(BF16)
        out_copy(c).start()

    def wait_work(c):
        act_wait(c)
        work(c)
        project(c)

    chunks(0, nc - 1, wait_work)
    act_wait(nc - 1)
    gp_send(0)
    work(nc - 1)

    def core_copy(h):
        rows = pl.ds(halves[h].start, halves[h].piece * halves[h].n_first)
        return remote(cs.at[rows], cr.at[rows], c_s.at[h], c_r.at[h], other)

    bias_core = remote(bacc, bcr, c_s.at[2], c_r.at[2], other)
    for h in range(2):
        rows = pl.ds(halves[h].start, halves[h].piece * halves[h].n_first)
        cs[rows] = acc[1 - core, rows].astype(BF16)
        core_copy(h).start()
    bias_core.start()
    project(nc - 1)

    zb = nz - 1

    def s1_copy(h, p, sender):
        return remote(s1s[h].at[p], s1r[h].at[sender], s1_s.at[h, p], s1_r.at[h, sender], first[h](p))

    def b1_copy(sender):
        return remote(bfin.at[0], b1r.at[sender], b1_s, b1_r.at[sender], z_peer(zb))

    for h in range(2):
        core_copy(h).wait_recv()
        hf = halves[h]

        def add_piece(p, h=h, hf=hf):
            rows = pl.ds(pl.multiple_of(hf.start + p * hf.piece, 16), hf.piece)
            total = acc[core, rows] + cr[rows].astype(F32)
            acc[core, rows] = total
            s1s[h][p] = total.astype(BF16)

        def add_send(p, h=h):
            add_piece(p)
            s1_copy(h, p, me_first[h]).start()

        ring(hf.n_first, me_first[h], add_send)
        add_piece(me_first[h])
    bias_core.wait_recv()
    bfin[0] = bacc[...] + bcr[...]
    gp_send(1)
    pl.when(z != zb)(lambda: b1_copy(z).start())

    def adjoint(c):
        pl.when(has_left)(lambda: gp_right(c).wait_recv())
        pl.when(has_right)(lambda: gp_left(c).wait_recv())
        grad = rows_dot_t(gp[c], taps[1]) + rows_dot_t(gpr[c], taps[0]) + rows_dot_t(gpl[c], taps[2])
        gsb[c] = (cot[c].astype(F32) + grad * slope[c]).astype(BF16)
        gsig_copy(c).start()

    def slice_of(p, n):
        return pl.ds(pl.multiple_of(p * n, 16), n)

    xb = NX - 1

    def x_copy(h, p, sender):
        return remote(xsb.at[h, slice_of(p, halves[h].owned)], xr[h].at[sender], x_s.at[h, p], x_r.at[h, sender], middle[h](p))

    def bx_copy(sender):
        return remote(bfin.at[0], bxr.at[sender], bx_s, bx_r.at[sender], x_peer(xb))

    for h in range(2):
        hf = halves[h]
        rows = pl.ds(pl.multiple_of(hf.start + me_first[h] * hf.piece, 16), hf.piece)
        pp[h, pl.ds(0, hf.piece)] = acc[core, rows]

        def take(p, h=h, hf=hf):
            s1_copy(h, me_first[h], p).wait_recv()
            pp[h, pl.ds(0, hf.piece)] += s1r[h][p].astype(F32)

        ring(hf.n_first, me_first[h], take)
        xsb[h, pl.ds(0, hf.piece)] = pp[h, pl.ds(0, hf.piece)].astype(BF16)

        def scatter(p, h=h, hf=hf):
            pl.when(p < hf.owners)(lambda: x_copy(h, p, me_middle[h]).start())

        ring(hf.n_middle, me_middle[h], scatter)

    @pl.when(z == zb)
    def _():
        def take_bias(p):
            b1_copy(p).wait_recv()
            bfin[0] += b1r[p]

        ring(nz, z, take_bias)
        pl.when(x != xb)(lambda: bx_copy(x).start())

    gp_send(2)

    def ar_copy(h, p, sender):
        return remote(ar[h].at[sender], ar[h].at[sender], ar_s.at[h, p], ar_r.at[h, sender], last[h](p))

    def bar_copy(p, sender):
        return remote(bar.at[sender], bar.at[sender], bar_s.at[p], bar_r.at[sender], y_peer(p))

    for h in range(2):
        hf = halves[h]

        @pl.when(me_middle[h] < hf.owners)
        def _(h=h, hf=hf):
            rows = slice_of(me_middle[h], hf.owned)

            def take(p):
                x_copy(h, me_middle[h], p).wait_recv()
                pp[h, rows] += xr[h][p].astype(F32)

            ring(hf.n_middle, me_middle[h], take)
            ar[h][me_last[h]] = pp[h, rows].astype(BF16)
            ring(hf.n_last, me_last[h], lambda p: ar_copy(h, p, me_last[h]).start())

    owns_bias = jnp.logical_and(z == zb, x == xb)

    @pl.when(owns_bias)
    def _():
        def take_bias(p):
            bx_copy(p).wait_recv()
            bfin[0] += bxr[p]

        ring(NX, x, take_bias)
        bar[y] = bfin[0]
        ring(ny, y, lambda p: bar_copy(p, y).start())

    def piece_of(h, p):
        return pl.ds(pl.multiple_of(halves[h].start + p * halves[h].piece, 16), halves[h].piece)

    def xg_copy(h, p, sender):
        n = halves[h].owned
        start = halves[h].start + me_first[h] * halves[h].piece + sender * n
        ref = gall.at[core, pl.ds(pl.multiple_of(start, 16), n)]
        return remote(ref, ref, xg_s.at[h, p], xg_r.at[h, sender], middle[h](p))

    def bxg_copy(p):
        return remote(bfin.at[1], bfin.at[1], bxg_s.at[p], bxg_r, x_peer(p))

    for h in range(2):
        hf = halves[h]

        @pl.when(me_middle[h] < hf.owners)
        def _(h=h, hf=hf):
            ring(hf.n_last, me_last[h], lambda p: ar_copy(h, me_last[h], p).wait_recv())
            total = ar[h][0].astype(F32)
            for p in range(1, hf.n_last):
                total = total + ar[h][p].astype(F32)
            start = hf.start + me_first[h] * hf.piece + me_middle[h] * hf.owned
            gall[core, pl.ds(pl.multiple_of(start, 16), hf.owned)] = total.astype(BF16)
            ring(hf.n_middle, me_middle[h], lambda p: xg_copy(h, p, me_middle[h]).start())

    @pl.when(owns_bias)
    def _():
        ring(ny, y, lambda p: bar_copy(y, p).wait_recv())
        total = bar[0]
        for p in range(1, ny):
            total = total + bar[p]
        bfin[1] = total
        ring(NX, x, lambda p: bxg_copy(p).start())

    gp_send(3)

    def ag1_copy(h, p, sender):
        ref = gall.at[core, piece_of(h, sender)]
        return remote(ref, ref, ag1_s.at[h, p], ag1_r.at[h, sender], first[h](p))

    def cag_copy(h, p, side):
        ref = gall.at[side, piece_of(h, p)]
        return remote(ref, ref, cag_s.at[h, p], cag_r.at[h, p], other)

    def bag_copy(p):
        return remote(bfin.at[1], bfin.at[1], bag_s.at[p], bag_r, z_peer(p))

    for h in range(2):
        hf = halves[h]

        def take(p, h=h, hf=hf):
            pl.when(p < hf.owners)(lambda: xg_copy(h, me_middle[h], p).wait_recv())

        ring(hf.n_middle, me_middle[h], take)
        ring(hf.n_first, me_first[h], lambda p, h=h: ag1_copy(h, p, me_first[h]).start())
        cag_copy(h, me_first[h], core).start()

    @pl.when(z == zb)
    def _():
        pl.when(x != xb)(lambda: bxg_copy(x).wait_recv())
        ring(nz, z, lambda p: bag_copy(p).start())

    chunks(0, nc - 2, adjoint)

    for h in range(2):
        hf = halves[h]

        def pass_on(p, h=h):
            ag1_copy(h, me_first[h], p).wait_recv()
            cag_copy(h, p, core).start()

        ring(hf.n_first, me_first[h], pass_on)
    def grad_copy(side):
        return pltpu.make_async_copy(gall.at[side], grads_h.at[side], w_sem.at[2 + side])

    grad_copy(core).start()
    chunks(nc - 2, nc, adjoint)
    pl.when(z != zb)(lambda: bag_copy(z).wait_recv())
    gbias_r[...] = jnp.sum(bfin[1], 0)
    for h in range(2):
        hf = halves[h]
        chunks(0, hf.n_first, lambda p, h=h: cag_copy(h, p, 1 - core).wait_recv())
    grad_copy(1 - core).start()

    def sent(c):
        @pl.when(has_right)
        def _():
            act_right(c).wait_send()
            gp_right(c).wait_send()

        @pl.when(has_left)
        def _():
            act_left(c).wait_send()
            gp_left(c).wait_send()

        out_copy(c).wait()
        gsig_copy(c).wait()

    chunks(0, nc, sent)
    bias_core.wait_send()
    pl.when(z != zb)(lambda: b1_copy(z).wait_send())
    pl.when(z == zb)(lambda: ring(nz, z, lambda p: bag_copy(p).wait_send()))
    for h in range(2):
        hf = halves[h]
        core_copy(h).wait_send()

        def sent_first(p, h=h):
            s1_copy(h, p, me_first[h]).wait_send()
            ag1_copy(h, p, me_first[h]).wait_send()

        ring(hf.n_first, me_first[h], sent_first)
        chunks(0, hf.n_first, lambda p, h=h: cag_copy(h, p, core).wait_send())

        def sent_x(p, h=h, hf=hf):
            pl.when(p < hf.owners)(lambda: x_copy(h, p, me_middle[h]).wait_send())

        ring(hf.n_middle, me_middle[h], sent_x)

        @pl.when(me_middle[h] < hf.owners)
        def _(h=h, hf=hf):
            ring(hf.n_middle, me_middle[h], lambda p: xg_copy(h, p, me_middle[h]).wait_send())
            ring(hf.n_last, me_last[h], lambda p: ar_copy(h, p, me_last[h]).wait_send())

    pl.when(jnp.logical_and(z == zb, x != xb))(lambda: bx_copy(x).wait_send())

    @pl.when(owns_bias)
    def _():
        ring(ny, y, lambda p: bar_copy(p, y).wait_send())
        ring(NX, x, lambda p: bxg_copy(p).wait_send())

    grad_copy(0).wait()
    grad_copy(1).wait()


def write_out(out_v, gsig_v, grads_v, gbias_v, out_h, gsig_h, gtaps_h, gbias_h, gout_h, sem):
    n_in = gtaps_h.shape[1]
    copies = [
        pltpu.make_async_copy(out_v, out_h, sem.at[0]),
        pltpu.make_async_copy(gsig_v, gsig_h, sem.at[1]),
        pltpu.make_async_copy(gbias_v, gbias_h, sem.at[2]),
    ]
    for k in range(4):
        part = grads_v.at[k // 2, pl.ds((k % 2) * n_in, n_in)]
        copies.append(pltpu.make_async_copy(part, gtaps_h.at[k] if k < 3 else gout_h, sem.at[3 + k]))
    for copy in copies:
        copy.start()
    for copy in copies:
        copy.wait()


def shards(sizes, signal, tap_weights, bias_inner, w_out, cotangent):
    n_seq, nyl = sizes
    nz, ny = n_seq // (2 * NYH * NX), NYH * nyl
    _, rows, c = signal.shape
    taps, _, hid = tap_weights.shape
    ch = CHUNK
    nc = rows // ch
    core_rows = (taps + 1) * c // 2
    share = SHARE * 8 // ny
    halves = (
        Half(0, share, ny, NX, nz),
        Half(share * ny, (core_rows - share * ny) // NX, NX, ny, nz),
    )
    cfg = (nz, ny, nyl, nc, ch, halves)
    any_spec = pl.BlockSpec(memory_space=pl.ANY)
    hbm_spec = pl.BlockSpec(memory_space=pltpu.HBM)
    vmem_spec = pl.BlockSpec(memory_space=pltpu.VMEM)
    block = lambda dtype: pltpu.VMEM((nc, ch, c), dtype)
    dma = lambda *shape: pltpu.SemaphoreType.DMA(shape)
    one = pltpu.SemaphoreType.DMA
    most = max(ny, nz, NX)
    scratch = [
        block(BF16), block(BF16), pltpu.VMEM(tap_weights.shape, BF16), pltpu.VMEM(w_out.shape, BF16),
        *[block(BF16)] * 9,
        block(F32), block(F32), block(F32),
        pltpu.VMEM((2, core_rows, hid), F32), pltpu.VMEM((8, hid), F32),
        pltpu.VMEM((core_rows, hid), BF16), pltpu.VMEM((core_rows, hid), BF16), pltpu.VMEM((8, hid), F32),
        *[pltpu.VMEM((h.n_first, h.piece, hid), BF16) for h in halves],
        *[pltpu.VMEM((h.n_first, h.piece, hid), BF16) for h in halves],
        pltpu.VMEM((nz, 8, hid), F32),
        pltpu.VMEM((NX, 8, hid), F32), pltpu.VMEM((ny, 8, hid), F32),
        pltpu.VMEM((2, max(h.piece for h in halves), hid), F32), pltpu.VMEM((2, max(h.piece for h in halves), hid), BF16),
        *[pltpu.VMEM((h.n_middle, h.owned, hid), BF16) for h in halves],
        *[pltpu.VMEM((h.n_last, h.owned, hid), BF16) for h in halves],
        pltpu.VMEM((2, 8, hid), F32),
        pltpu.VMEM((2, core_rows, hid), BF16),
        dma(2 * nc), dma(6), dma(2 * nc),
        dma(2 * nc), dma(2 * nc), dma(2 * nc), dma(2 * nc),
        dma(3), dma(3), dma(2, most), dma(2, most), one, dma(nz), one, dma(NX), dma(ny), dma(ny), dma(NX), one,
        *[dma(2, most)] * 8,
        dma(nz), one, dma(2, most), dma(2, most),
    ]
    in_hbm = lambda value: pltpu.with_memory_space_constraint(value, pltpu.HBM)
    results = pl.pallas_call(
        functools.partial(kernel, cfg),
        out_shape=(
            pltpu.VMEM(signal.shape, BF16),
            pltpu.VMEM(signal.shape, BF16),
            pltpu.VMEM((2, core_rows, hid), BF16),
            pltpu.VMEM((hid,), F32),
        ),
        in_specs=[hbm_spec, hbm_spec, vmem_spec, hbm_spec, hbm_spec],
        out_specs=(any_spec, any_spec, any_spec, vmem_spec),
        scratch_shapes=scratch,
        compiler_params=pltpu.CompilerParams(collective_id=0, has_side_effects=True, vmem_limit_bytes=40 * 1024 * 1024),
    )(in_hbm(signal), in_hbm(tap_weights), in_hbm(bias_inner), in_hbm(w_out), in_hbm(cotangent))
    return pl.pallas_call(
        write_out,
        out_shape=(
            jax.ShapeDtypeStruct(signal.shape, BF16),
            jax.ShapeDtypeStruct(signal.shape, BF16),
            jax.ShapeDtypeStruct(tap_weights.shape, BF16),
            jax.ShapeDtypeStruct((hid,), F32),
            jax.ShapeDtypeStruct(w_out.shape, BF16),
        ),
        in_specs=[any_spec] * 4,
        out_specs=(hbm_spec,) * 5,
        scratch_shapes=[dma(7)],
        compiler_params=pltpu.CompilerParams(vmem_limit_bytes=8 * 1024 * 1024),
    )(*[pltpu.with_memory_space_constraint(value, pltpu.VMEM) for value in results])


def solution(mesh):
    sizes = (mesh.shape["seq"], mesh.shape["grp"])
    return jax.shard_map(
        functools.partial(shards, sizes),
        mesh=mesh,
        in_specs=(P("grp", "seq", None), P(), P(), P(), P("grp", "seq", None)),
        out_specs=(P("grp", "seq", None), P("grp", "seq", None), P(), P(), P()),
        check_vma=False,
    )
```
